32 devices in a mesh: ctx: 16 (over z, y, core), fsdp: 2 (over x).
Axes of the slice: x: 2, y: 2, z: 4, core: 2. Of those that a mesh axis runs over, the one named last changes fastest.
Arguments:
- inputs: bfloat16 [4, 8192, 1024], P('fsdp', 'ctx'), may hold values from -6 to 6
- cotangent: bfloat16 [4, 8192, 1024], P('fsdp', 'ctx'), may hold values from -6 to 6
- segments: int32 [4, 8192], P('fsdp'), may hold values from 0 to 7, as said below
- w_qkv: bfloat16 [1024, 3072], P('fsdp'), may hold values from -0.25 to 0.25
- w_out: bfloat16 [1024, 1024], P('fsdp'), may hold values from -0.75 to 0.75
- w_in: bfloat16 [1024, 5248], P('fsdp'), may hold values from -0.1875 to 0.1875
- w_down: bfloat16 [2624, 1024], P('fsdp'), may hold values from -0.125 to 0.125
- norm_gains: bfloat16 [2, 1024], P(None, 'fsdp'), may hold values from 0.5 to 1.5
- slot_table: int32 [2992], replicated, may hold values from 0 to 3007, as said below
- master: float32 [3008, 64, 64], P(('ctx', 'fsdp')), may hold values from -0.1875 to 0.1875
- first_moment: float32 [3008, 64, 64], P(('ctx', 'fsdp'))
- rotated_second_moments: float32 [3008, 64, 64], P(('ctx', 'fsdp')), may hold values from 16384 to 65536
- row_eigenbasis: float32 [3008, 64, 64], P(('ctx', 'fsdp')), may hold values from -0.75 to 0.75
- column_eigenbasis: float32 [3008, 64, 64], P(('ctx', 'fsdp')), may hold values from -0.75 to 0.75
- gain_master: float32 [2, 1024], replicated, may hold values from 0.5 to 1.5
- gain_first: float32 [2, 1024], replicated
- gain_second: float32 [2, 1024], replicated, may hold values from 16384 to 65536
Outputs:
- layer_out: bfloat16 [4, 8192, 1024], P('fsdp', 'ctx')
- input_grad: bfloat16 [4, 8192, 1024], P('fsdp', 'ctx')
- block_grads: float32 [3008, 64, 64], P(('ctx', 'fsdp'))
- gain_grads: float32 [2, 1024], replicated
- new_master: float32 [3008, 64, 64], P(('ctx', 'fsdp'))
- new_copy: bfloat16 [3008, 64, 64], P(('ctx', 'fsdp'))
- new_first: float32 [3008, 64, 64], P(('ctx', 'fsdp'))
- new_second: float32 [3008, 64, 64], P(('ctx', 'fsdp'))
- new_gains: float32 [2, 1024], replicated
- new_gain_first: float32 [2, 1024], replicated
- new_gain_second: float32 [2, 1024], replicated
The draws below stay inside these ranges and needn't reach their ends.
Inputs may be any that keep to these rules, and one draw needn't show every extreme that they name: `segments`: document numbers never fall along a sequence; each sequence holds 8 documents of one or more positions each, exactly one of them 8192 // 2 positions long. `slot_table`: distinct slots; device r of ctx+fsdp (ctx the slower) holds slots r * 94 to r * 94 + 93; slots 0 and 3007 are in use.
All inputs are finite; a program needn't handle non-finite values.
Results may differ from the reference program's by a relative error of at most 0.02.
Values may be sent and summed in bfloat16 or wider, within the bound.
No kernel may reach another device: no remote copies, remote signals or barrier semaphores. Data moves between devices by JAX's collectives and lax.ppermute only.
A program may use at most 448 MiB of HBM per device.

```python
import math
import jax
import jax.numpy as jnp
from jax import lax

MODEL_WIDTH = 1024
HEADS = 16
HEAD = 64
FF = 2624
SEQ_LEN = 8192
NDOC = 8
BLOCK_ORDER = 64
SEQS = 4
TOKENS = 32768
MATRIX_BLOCKS = 2992
SLOT_COUNT = 3008


def document_lengths(key):
    seq_keys = jax.random.split(key, SEQS)

    def one_sequence(seq_key):
        key_exp, key_mult, key_long = jax.random.split(seq_key, 3)
        powers = jax.random.randint(key_exp, (NDOC,), 0, 8)
        weights = jnp.left_shift(jnp.ones_like(powers), powers) * jax.random.randint(key_mult, (NDOC,), 1, 4)
        long_doc = jax.random.randint(key_long, (), 0, NDOC)
        doc_ids = jnp.arange(NDOC, dtype=jnp.int32)
        others = doc_ids != long_doc
        weights = jnp.where(others, weights, 0)
        total_weight = jnp.sum(weights)
        rest_len = SEQ_LEN - SEQ_LEN // 2
        spare_len = rest_len - (NDOC - 1)
        base_len = jnp.where(others, 1 + spare_len * weights // total_weight, SEQ_LEN // 2)
        leftover = rest_len - jnp.sum(jnp.where(others, base_len, 0))
        first_other = jnp.where(long_doc == 0, 1, 0)
        base_len = base_len + jnp.where(doc_ids == first_other, leftover, 0)
        return base_len.astype(jnp.int32)
    return jax.vmap(one_sequence)(seq_keys)


def draw_segments(key, part):
    doc_lengths = document_lengths(jax.random.fold_in(key, 11))
    doc_ends = jnp.cumsum(doc_lengths, axis=1)
    places = jnp.arange(SEQ_LEN, dtype=jnp.int32)
    return jnp.sum((places[None, :, None] >= doc_ends[:, None, :]).astype(jnp.int32), axis=2).astype(jnp.int32)


def draw_slot_table(key, part):
    key_selection, key_order = jax.random.split(jax.random.fold_in(key, 23))
    middle_value = (jax.random.permutation(key_selection, SLOT_COUNT - 2)[:MATRIX_BLOCKS - 2] + 1).astype(jnp.int32)
    picked_entry = jnp.concatenate([jnp.zeros((1,), jnp.int32), jnp.full((1,), SLOT_COUNT - 1, jnp.int32), middle_value])
    return jax.random.permutation(key_order, picked_entry).astype(jnp.int32)


def draw_first_moment(key, part):
    normal_component = jax.random.truncated_normal(jax.random.fold_in(key, 31), -4.0, 4.0, (SLOT_COUNT, BLOCK_ORDER, BLOCK_ORDER), jnp.float32)
    return normal_component * jnp.sqrt(TOKENS * 1.0)


def draw_gain_first(key, part):
    normal_component = jax.random.truncated_normal(jax.random.fold_in(key, 37), -4.0, 4.0, (2, MODEL_WIDTH), jnp.float32)
    return normal_component * jnp.sqrt(TOKENS * 1.0)


def shard_levels(stream_key, extent, cuts, low, largest):
    gain, own = 1.0, jax.random.fold_in(stream_key, 6)
    for dim, parts in cuts:
        draws = jnp.exp(jax.random.uniform(jax.random.fold_in(own, dim), (parts,), jnp.float32, low / len(cuts), largest / len(cuts)))
        gain = gain * jnp.repeat(draws, extent[dim] // parts).reshape([-1 if axis == dim else 1 for axis in range(len(extent))])
    return gain


def gaussian(own_key, dims, deviation, limit, shards=(), kind=jnp.bfloat16):
    values = deviation * jax.random.normal(own_key, dims, jnp.float32)
    if shards:
        values = values * shard_levels(own_key, dims, shards, -0.22, 0.18)
    return jnp.clip(values, -limit, limit).astype(kind)


def setup_inputs(seed: int = 0) -> dict:
    streams_of = jax.random.split(jax.random.key(seed), 18)
    return {
        "inputs": gaussian(streams_of[0], (SEQS, SEQ_LEN, MODEL_WIDTH), 1.0, 6.0, ((0, 2), (1, 16))),
        "cotangent": gaussian(streams_of[1], (SEQS, SEQ_LEN, MODEL_WIDTH), 1.0, 6.0, ((0, 2), (1, 16))),
        "segments": draw_segments(jax.random.fold_in(streams_of[17], 71), 0),
        "w_qkv": gaussian(streams_of[3], (MODEL_WIDTH, 3 * MODEL_WIDTH), (MODEL_WIDTH // 2) ** -0.5, 0.25, ((0, 2),)),
        "w_out": gaussian(streams_of[4], (MODEL_WIDTH, MODEL_WIDTH), HEAD ** -0.5, 0.75, ((0, 2),)),
        "w_in": gaussian(streams_of[5], (MODEL_WIDTH, 2 * FF), MODEL_WIDTH ** -0.5, 0.1875, ((0, 2),)),
        "w_down": gaussian(streams_of[6], (FF, MODEL_WIDTH), FF ** -0.5, 0.125, ((0, 2),)),
        "norm_gains": jnp.clip(1.0 + 0.1 * jax.random.normal(streams_of[7], (2, MODEL_WIDTH), jnp.float32), 0.5, 1.5).astype(jnp.bfloat16),
        "slot_table": draw_slot_table(jax.random.fold_in(streams_of[17], 71), 0),
        "master": gaussian(streams_of[9], (SLOT_COUNT, BLOCK_ORDER, BLOCK_ORDER), MODEL_WIDTH ** -0.5, 0.1875, ((0, 32),), jnp.float32),
        "first_moment": draw_first_moment(jax.random.fold_in(streams_of[17], 71), 0),
        "rotated_second_moments": jnp.clip(jnp.exp(math.log(65536.0) - 1.3862944 * jax.random.uniform(streams_of[11], (SLOT_COUNT, BLOCK_ORDER, BLOCK_ORDER), jnp.float32) ** shard_levels(streams_of[11], (SLOT_COUNT, BLOCK_ORDER, BLOCK_ORDER), ((0, 32),), -0.2, 0.2)), 16384.0, 65536.0),
        "row_eigenbasis": gaussian(streams_of[12], (SLOT_COUNT, BLOCK_ORDER, BLOCK_ORDER), BLOCK_ORDER ** -0.5, 0.75, ((0, 32),), jnp.float32),
        "column_eigenbasis": gaussian(streams_of[13], (SLOT_COUNT, BLOCK_ORDER, BLOCK_ORDER), BLOCK_ORDER ** -0.5, 0.75, ((0, 32),), jnp.float32),
        "gain_master": jnp.clip(1.0 + 0.1 * jax.random.normal(streams_of[14], (2, MODEL_WIDTH), jnp.float32), 0.5, 1.5),
        "gain_first": draw_gain_first(jax.random.fold_in(streams_of[17], 71), 0),
        "gain_second": jnp.clip(jnp.exp(jax.random.uniform(streams_of[16], (2, MODEL_WIDTH), jnp.float32, math.log(16384.0), math.log(65536.0))), 16384.0, 65536.0),
    }


@jax.custom_vjp
def low(v):
    return lax.optimization_barrier(v.astype(jnp.bfloat16)).astype(jnp.float32)

@jax.custom_vjp
def low_back(v):
    return v

def low_keep(v):
    return (low(v), None)

def low_pass(kept, grad):
    return (grad,)

def back_keep(v):
    return (v, None)

def back_low(kept, grad):
    return (low(grad),)
low.defvjp(low_keep, low_pass)
low_back.defvjp(back_keep, back_low)
highest = lax.Precision.HIGHEST
rope_base = 160000.0
norm_eps = 1e-05
adam_eps = 1e-08
beta_one = 0.5
beta_two = 0.5
block_rate = 0.03
gain_rate = 0.75
decay_rate = 0.01
masked_score = -1e+30

def layer_norm(values, gain_row):
    center = values - lax.optimization_barrier(jnp.mean(values, axis=-1, keepdims=True))
    spread = lax.optimization_barrier(jnp.mean(center * center, axis=-1, keepdims=True))
    return center * lax.rsqrt(spread + norm_eps) * gain_row

def rope_tables(positions, head_size):
    half_size = head_size // 2
    frequency = rope_base ** (-(jnp.arange(half_size, dtype=jnp.float32) * 2.0) / head_size)
    angles = positions.astype(jnp.float32)[:, None] * frequency[None, :]
    angles = jnp.concatenate([angles, angles], axis=1)
    return (jnp.cos(angles)[:, None, :], jnp.sin(angles)[:, None, :])

def rotate_pairs(heads_in, cosine, sine_rows):
    half_size = heads_in.shape[-1] // 2
    turned = jnp.concatenate([-heads_in[..., half_size:], heads_in[..., :half_size]], axis=-1)
    return heads_in * cosine + turned * sine_rows

def doc_positions(seg_row):
    doc_ids = jnp.arange(NDOC, dtype=jnp.int32)
    matches = seg_row[:, None] == doc_ids[None, :]
    counts = lax.optimization_barrier(jnp.sum(matches.astype(jnp.int32), axis=0)).astype(jnp.int32)
    starts = (jnp.cumsum(counts) - counts).astype(jnp.int32)
    doc_begin = lax.optimization_barrier(jnp.sum(jnp.where(matches, starts[None, :], 0), axis=1)).astype(jnp.int32)
    return (jnp.arange(seg_row.shape[0], dtype=jnp.int32) - doc_begin).astype(jnp.int32)

def gated_gelu(gate_up):
    return jax.nn.gelu(gate_up[:, :FF], approximate=False) * gate_up[:, FF:]

def attend_sequence(queries, keys_rot, values, seg_row):
    full_len = queries.shape[0]
    query_block = min(512, full_len)
    block_count = full_len // query_block
    score_scale = HEAD ** (-0.5)

    def one_block(pieces):
        block_queries, block_segs = pieces
        raw_scores = jnp.einsum('qhe,khe->hqk', block_queries, keys_rot, precision=highest) * score_scale
        raw_scores = low_back(raw_scores)
        same_doc = (block_segs[:, None] == seg_row[None, :])[None, :, :]
        masked = jnp.where(same_doc, raw_scores, masked_score)
        shifted = jnp.exp(masked - lax.optimization_barrier(jnp.max(masked, axis=2, keepdims=True)))
        prob_full = shifted / lax.optimization_barrier(jnp.sum(shifted, axis=2, keepdims=True))
        return jnp.einsum('hqk,khe->qhe', low(prob_full), values, precision=highest)
    blocks = lax.map(jax.checkpoint(one_block), (queries.reshape(block_count, query_block, HEADS, HEAD), seg_row.reshape(block_count, query_block)))
    return blocks.reshape(full_len, HEADS, HEAD)

def forward_sequence(param_set, layer_in, seg_row, pos_row):
    w_qkv, w_out, w_in, w_down, norm_gains = param_set
    full_len = layer_in.shape[0]
    normed = low(layer_norm(layer_in, norm_gains[0]))
    projected = low_back(jnp.dot(normed, w_qkv, precision=highest)).reshape(full_len, 3, HEADS, HEAD)
    cosine, sine_rows = rope_tables(pos_row, HEAD)
    queries = low(rotate_pairs(projected[:, 0], cosine, sine_rows))
    keys_rot = low(rotate_pairs(projected[:, 1], cosine, sine_rows))
    values = low(projected[:, 2])
    attended = attend_sequence(queries, keys_rot, values, seg_row).reshape(full_len, MODEL_WIDTH)
    attended = low(low_back(attended))
    middle_value = layer_in + low_back(jnp.dot(attended, w_out, precision=highest))
    normed_two = low(layer_norm(middle_value, norm_gains[1]))
    gate_up = low_back(jnp.dot(normed_two, w_in, precision=highest))
    hidden = low(gated_gelu(gate_up))
    return middle_value + low_back(jnp.dot(hidden, w_down, precision=highest))

def to_blocks(matrix):
    row_count, col_count = matrix.shape
    tiled = matrix.reshape(row_count // BLOCK_ORDER, BLOCK_ORDER, col_count // BLOCK_ORDER, BLOCK_ORDER).transpose(0, 2, 1, 3)
    return tiled.reshape(-1, BLOCK_ORDER, BLOCK_ORDER)

def soap_step(grads_in, weights_old, first_old, second_old, left_side, right_side):
    turned = jnp.einsum('bji,bjk->bik', left_side, grads_in, precision=highest)
    turned = jnp.einsum('bik,bkl->bil', turned, right_side, precision=highest)
    first_new = beta_one * first_old + (1.0 - beta_one) * turned
    second_new = beta_two * second_old + (1.0 - beta_two) * turned * turned
    normal_step = first_new / (jnp.sqrt(second_new) + adam_eps)
    restored = jnp.einsum('bij,bjk->bik', left_side, normal_step, precision=highest)
    restored = jnp.einsum('bik,blk->bil', restored, right_side, precision=highest)
    weights_new = weights_old - block_rate * (restored + decay_rate * weights_old)
    return (weights_new, first_new, second_new)

def gain_step(grads_in, gains_old, first_old, second_old):
    first_new = beta_one * first_old + (1.0 - beta_one) * grads_in
    second_new = beta_two * second_old + (1.0 - beta_two) * grads_in * grads_in
    gains_new = gains_old - gain_rate * first_new / (jnp.sqrt(second_new) + adam_eps)
    return (gains_new, first_new, second_new)

def reference(inputs, cotangent, segments, w_qkv, w_out, w_in, w_down, norm_gains, slot_table, master, first_moment, rotated_second_moments, row_eigenbasis, column_eigenbasis, gain_master, gain_first, gain_second):
    positions = jax.vmap(doc_positions)(segments)
    param_set = (w_qkv.astype(jnp.float32), w_out.astype(jnp.float32), w_in.astype(jnp.float32), w_down.astype(jnp.float32), norm_gains.astype(jnp.float32))

    def whole_layer(params_in, layer_in):
        return lax.map(lambda pieces: forward_sequence(params_in, pieces[0], pieces[1], pieces[2]), (layer_in, segments, positions))
    layer_f32, pullback = jax.vjp(whole_layer, param_set, inputs.astype(jnp.float32))
    param_grads, input_f32 = pullback(cotangent.astype(jnp.float32))
    tiles = jnp.concatenate([to_blocks(param_grads[0]), to_blocks(param_grads[1]), to_blocks(param_grads[2]), to_blocks(param_grads[3])], axis=0)
    block_grads = jnp.zeros(master.shape, jnp.float32).at[slot_table].set(tiles)
    weights_new, first_new, second_new = soap_step(tiles, master[slot_table], first_moment[slot_table], rotated_second_moments[slot_table], row_eigenbasis[slot_table], column_eigenbasis[slot_table])
    new_master = master.at[slot_table].set(weights_new)
    new_first = first_moment.at[slot_table].set(first_new)
    new_second = rotated_second_moments.at[slot_table].set(second_new)
    gain_grads = param_grads[4]
    new_gains, new_gain_first, new_gain_second = gain_step(gain_grads, gain_master, gain_first, gain_second)
    return (layer_f32.astype(jnp.bfloat16), input_f32.astype(jnp.bfloat16), block_grads, gain_grads, new_master, new_master.astype(jnp.bfloat16), new_first, new_second, new_gains, new_gain_first, new_gain_second)
```

```python
import functools
import jax, jax.numpy as jnp
from jax import lax
from jax.experimental import pallas as pl
from jax.experimental.pallas import tpu as pltpu
from jax.sharding import PartitionSpec as P

HEAD = 64
NDOC=8
BIG=1e30
LN2=0.6931471805599453
LOG2E=1.4426950408889634

def split3(v):
    hi=v.astype(jnp.bfloat16)
    r=v-hi.astype(jnp.float32)
    mid=r.astype(jnp.bfloat16)
    lo=(r-mid.astype(jnp.float32)).astype(jnp.bfloat16)
    return hi.astype(jnp.float32),mid.astype(jnp.float32),lo.astype(jnp.float32)

def doc_rows(seg_row):
    n=seg_row.shape[1]
    ids=lax.broadcasted_iota(jnp.int32,(NDOC,n),0)
    return (ids==seg_row).astype(jnp.float32)

def fwd_kernel(bq,bk,sub,lo_ref,hi_ref,qkv_ref,seg_ref,out_ref,raw_ref,lse_ref,q_s,k_s,v_s):
    chunks,_,width=qkv_ref.shape
    full=chunks*width
    def prep(c,carry):
        cols=pl.ds(pl.multiple_of(c*width,width),width)
        hot=doc_rows(seg_ref[:,cols])
        zero8=jnp.zeros((8,width),jnp.float32)
        q_s[0:64,cols]=qkv_ref[c,0:64,:]
        q_s[64:80,cols]=jnp.concatenate([hot,zero8],0).astype(jnp.bfloat16)
        kt=jnp.concatenate([qkv_ref[c,64:128,:].astype(jnp.float32),(hot-1.0)*BIG,jnp.zeros((56,width),jnp.float32)],0)
        k_s[cols,:]=kt.T.astype(jnp.bfloat16)
        v_s[0:64,cols]=qkv_ref[c,128:192,:]
        row=lax.broadcasted_iota(jnp.int32,(16,width),0)
        v_s[64:80,cols]=(row==0).astype(jnp.bfloat16)
        return carry
    lax.fori_loop(0,chunks,prep,0)
    def q_step(i,carry):
        cols=pl.ds(pl.multiple_of(i*bq,bq),bq)
        qa=q_s[:,cols]
        def k_step(j,state):
            rows=pl.ds(pl.multiple_of(j*bk,bk),bk)
            ka=k_s[rows,0:80]
            va=v_s[:,rows]
            new=[]
            for n in range(bq//sub):
                m,acc=state[n]
                s=jnp.dot(ka,qa[:,n*sub:(n+1)*sub],preferred_element_type=jnp.float32)
                m_new=jnp.maximum(m,jnp.max(s,axis=0,keepdims=True))
                p=jnp.exp2(s-m_new).astype(jnp.bfloat16)
                acc=acc*jnp.exp2(m-m_new)+jnp.dot(va,p,preferred_element_type=jnp.float32)
                new.append((m_new,acc))
            return tuple(new)
        init=tuple((jnp.full((1,sub),-3e38,jnp.float32),jnp.zeros((80,sub),jnp.float32)) for _ in range(bq//sub))
        state=lax.fori_loop(lo_ref[i],hi_ref[i],k_step,init)
        m=jnp.concatenate([s[0] for s in state],1); acc=jnp.concatenate([s[1] for s in state],1)
        total=acc[64:65]
        o=acc[0:64]/total
        raw_ref[:,cols]=o
        lse_ref[:,cols]=m+jnp.log2(total)
        return carry
    lax.fori_loop(0,full//bq,q_step,0)
    def emit(c,carry):
        cols=pl.ds(pl.multiple_of(c*width,width),width)
        out_ref[c]=raw_ref[:,cols].astype(jnp.bfloat16)
        return carry
    lax.fori_loop(0,chunks,emit,0)

def bwd_kernel(bq,bk,sub,lo_ref,hi_ref,qkv_ref,seg_ref,do_ref,raw_ref,lse_ref,cos_ref,sin_ref,out_ref,
               q_s,k_s,kt_s,v_s,do_s,qd_s,dkv_s):
    chunks,_,width=qkv_ref.shape
    full=chunks*width
    def prep(c,carry):
        cols=pl.ds(pl.multiple_of(c*width,width),width)
        hot=doc_rows(seg_ref[:,cols])
        row=lax.broadcasted_iota(jnp.int32,(8,width),0)
        ones3=(row<3).astype(jnp.float32)
        def three(v):
            a,b,d=split3(-v)
            return jnp.where(row==0,a,jnp.where(row==1,b,jnp.where(row==2,d,0.0)))
        qt=qkv_ref[c,0:64,:]
        q_s[0:64,cols]=qt
        q_s[64:80,cols]=jnp.concatenate([hot,three(lse_ref[:,cols])],0).astype(jnp.bfloat16)
        kt=qkv_ref[c,64:128,:]
        kt_s[:,cols]=kt
        vt=qkv_ref[c,128:192,:]
        kk=jnp.concatenate([kt.astype(jnp.float32),(hot-1.0)*BIG,ones3,jnp.zeros((48,width),jnp.float32)],0)
        k_s[cols,:]=kk.T.astype(jnp.bfloat16)
        vv=jnp.concatenate([vt.astype(jnp.float32),ones3,jnp.zeros((56,width),jnp.float32)],0)
        v_s[cols,:]=vv.T.astype(jnp.bfloat16)
        dot_=do_ref[c].astype(jnp.float32)
        delta=jnp.sum(dot_*raw_ref[:,cols],axis=0,keepdims=True)
        do_s[0:64,cols]=do_ref[c]
        do_s[64:80,cols]=jnp.concatenate([three(delta),jnp.zeros((8,width),jnp.float32)],0).astype(jnp.bfloat16)
        z=jnp.zeros((64,width),jnp.float32)
        qd_s[0,cols,:]=jnp.concatenate([qt.astype(jnp.float32),z],0).T.astype(jnp.bfloat16)
        qd_s[1,cols,:]=jnp.concatenate([z,dot_],0).T.astype(jnp.bfloat16)
        dkv_s[cols,:]=jnp.zeros((width,128),jnp.float32)
        return carry
    lax.fori_loop(0,chunks,prep,0)
    per=width//bq
    def q_step(i,carry):
        cols=pl.ds(pl.multiple_of(i*bq,bq),bq)
        qa=q_s[:,cols]; da=do_s[:,cols]; qn=qd_s[0,cols,:]; dn=qd_s[1,cols,:]
        def k_step(j,accs):
            rows=pl.ds(pl.multiple_of(j*bk,bk),bk)
            new=list(accs)
            for r in range(bk//sub):
                rr=pl.ds(pl.multiple_of(j*bk+r*sub,sub),sub)
                s=jnp.dot(k_s[rr,0:80],qa,preferred_element_type=jnp.float32)
                dp=jnp.dot(v_s[rr,0:80],da,preferred_element_type=jnp.float32)
                p=jnp.exp2(s)
                p16=p.astype(jnp.bfloat16)
                ds=(p*dp).astype(jnp.bfloat16)
                dkv_s[rr,:]+=jnp.dot(ds,qn,preferred_element_type=jnp.float32)+jnp.dot(p16,dn,preferred_element_type=jnp.float32)
                new[0]=new[0]+jnp.dot(kt_s[:,rr],ds,preferred_element_type=jnp.float32)
            return tuple(new)
        (dq,)=lax.fori_loop(lo_ref[i],hi_ref[i],k_step,(jnp.zeros((64,bq),jnp.float32),))
        dq=dq*0.125
        c=cos_ref[:,cols]; s=sin_ref[:,cols]
        a,b=dq[0:32],dq[32:64]
        rot=jnp.concatenate([a*c+b*s,b*c-a*s],0).astype(jnp.bfloat16)
        out_ref[i//per,0:64,pl.ds(pl.multiple_of((i%per)*bq,bq),bq)]=rot
        return carry
    lax.fori_loop(0,full//bq,q_step,0)
    def emit(c,carry):
        cols=pl.ds(pl.multiple_of(c*width,width),width)
        t=dkv_s[cols,:].T
        dk=t[0:64]*LN2
        co=cos_ref[:,cols]; si=sin_ref[:,cols]
        a,b=dk[0:32],dk[32:64]
        out_ref[c,64:192,:]=jnp.concatenate([a*co+b*si,b*co-a*si,t[64:128]],0).astype(jnp.bfloat16)
        return carry
    lax.fori_loop(0,chunks,emit,0)

def ranges(seg_row,bq,bk):
    full=seg_row.shape[0]
    firsts=seg_row[::bq]; lasts=seg_row[bq-1::bq]
    lo=jnp.sum((seg_row[None,:]<firsts[:,None]).astype(jnp.int32),axis=1)//bk
    hi=-(-jnp.sum((seg_row[None,:]<=lasts[:,None]).astype(jnp.int32),axis=1)//bk)
    return lo.astype(jnp.int32),hi.astype(jnp.int32)

VM=pl.BlockSpec(memory_space=pltpu.VMEM)
SM=pl.BlockSpec(memory_space=pltpu.SMEM)
def attend_forward(qkv,seg_row,bq=512,bk=512,sub=256):
    chunks,_,width=qkv.shape; full=chunks*width
    lo,hi=ranges(seg_row,bq,bk)
    return pl.pallas_call(functools.partial(fwd_kernel,bq,bk,sub),
      out_shape=(jax.ShapeDtypeStruct((chunks,64,width),jnp.bfloat16),jax.ShapeDtypeStruct((64,full),jnp.float32),jax.ShapeDtypeStruct((1,full),jnp.float32)),
      in_specs=[SM,SM,VM,VM],out_specs=(VM,VM,VM),
      scratch_shapes=[pltpu.VMEM((80,full),jnp.bfloat16),pltpu.VMEM((full,128),jnp.bfloat16),pltpu.VMEM((80,full),jnp.bfloat16)],
      compiler_params=pltpu.CompilerParams(vmem_limit_bytes=40<<20),
      cost_estimate=pl.CostEstimate(flops=4*64*full*full//3,bytes_accessed=8<<20,transcendentals=full*full//3),
      name="attend_fwd")(lo,hi,qkv,seg_row[None,:])
def attend_backward(qkv,seg_row,do,raw,lse,cos,sin,bq=512,bk=512,sub=512):
    chunks,_,width=qkv.shape; full=chunks*width
    lo,hi=ranges(seg_row,bq,bk)
    return pl.pallas_call(functools.partial(bwd_kernel,bq,bk,sub),
      out_shape=jax.ShapeDtypeStruct((chunks,192,width),jnp.bfloat16),
      in_specs=[SM,SM,VM,VM,VM,VM,VM,VM,VM],out_specs=VM,
      scratch_shapes=[pltpu.VMEM((80,full),jnp.bfloat16),pltpu.VMEM((full,128),jnp.bfloat16),pltpu.VMEM((64,full),jnp.bfloat16),
        pltpu.VMEM((full,128),jnp.bfloat16),pltpu.VMEM((80,full),jnp.bfloat16),pltpu.VMEM((2,full,128),jnp.bfloat16),pltpu.VMEM((full,128),jnp.float32)],
      compiler_params=pltpu.CompilerParams(vmem_limit_bytes=56<<20),
      cost_estimate=pl.CostEstimate(flops=10*64*full*full//3,bytes_accessed=16<<20,transcendentals=full*full//3),
      name="attend_bwd")(lo,hi,qkv,seg_row[None,:],do,raw,lse,cos,sin)

FF = 2624
BLOCK_ORDER = 64
rope_base = 160000.0
norm_eps = 1e-05
adam_eps = 1e-08
beta_one = 0.5
beta_two = 0.5
block_rate = 0.03
gain_rate = 0.75
decay_rate = 0.01
BF = jnp.bfloat16
F32 = jnp.float32


def layer_norm(values, gain_row):
    center = values - jnp.mean(values, axis=-1, keepdims=True)
    spread = jnp.mean(center * center, axis=-1, keepdims=True)
    return center * lax.rsqrt(spread + norm_eps) * gain_row


def norm_back(values, gain_row, grad_rows):
    unused, pullback = jax.vjp(layer_norm, values, gain_row)
    return pullback(grad_rows)


def doc_positions(seg_row):
    doc_ids = jnp.arange(NDOC, dtype=jnp.int32)
    matches = seg_row[:, None] == doc_ids[None, :]
    counts = jnp.sum(matches.astype(jnp.int32), axis=0)
    starts = jnp.cumsum(counts) - counts
    doc_begin = jnp.sum(jnp.where(matches, starts[None, :], 0), axis=1)
    return jnp.arange(seg_row.shape[0], dtype=jnp.int32) - doc_begin


def rope_tables(positions):
    half = HEAD // 2
    frequency = rope_base ** (-(jnp.arange(half, dtype=F32) * 2.0) / HEAD)
    angles = positions.astype(F32)[None, :] * frequency[:, None]
    return jnp.cos(angles), jnp.sin(angles)


def gated_gelu(gate_up):
    return jax.nn.gelu(gate_up[:, :FF], approximate=False) * gate_up[:, FF:]


def gated_both(gate_up, grad_hidden):
    hidden, pullback = jax.vjp(gated_gelu, gate_up)
    return hidden, pullback(grad_hidden)[0]


def mm(a, b, da, db):
    return lax.dot_general(a, b, (((da,), (db,)), ((), ())), preferred_element_type=F32)


def swap_bit(x, axis, bit):
    n = lax.axis_size(axis)
    return lax.ppermute(x, axis, [(s, s ^ bit) for s in range(n)])


def gather_rows(shard, axis_name="fsdp"):
    if lax.axis_size(axis_name) != 2 or lax.axis_size("ctx") % 2:
        return lax.all_gather(shard, axis_name, axis=0, tiled=True)
    rows = shard.shape[0]
    core = lax.axis_index("ctx") % 2
    half = rows // 2
    piece = lax.dynamic_slice_in_dim(shard, core * half, half)
    got = swap_bit(piece, axis_name, 1)
    twin = swap_bit(got, "ctx", 1)
    first = core == 0
    mine = lax.axis_index(axis_name) == 0
    low = jnp.where(first, got, twin)
    high = jnp.where(first, twin, got)
    other = jnp.concatenate([low, high], axis=0)
    return jnp.concatenate([jnp.where(mine, shard, other), jnp.where(mine, other, shard)], axis=0)


def reduce_parts(blocks):
    ctx_size, fsdp_size = lax.axis_size("ctx"), lax.axis_size("fsdp")
    ctx_bits = ctx_size.bit_length() - 1
    fsdp_bits = fsdp_size.bit_length() - 1
    cap = blocks.shape[0] // (ctx_size * fsdp_size)
    tail = blocks.shape[1:]
    names = [("ctx", 1 << b) for b in reversed(range(ctx_bits))] + [
        ("fsdp", 1 << b) for b in reversed(range(fsdp_bits))
    ]
    x = blocks.reshape((2,) * len(names) + (cap,) + tail)

    def halve(x, left, key):
        axis = left.index(key)
        mine = jnp.bitwise_and(lax.axis_index(key[0]), key[1]) // key[1]
        keep = lax.dynamic_index_in_dim(x, mine, axis, keepdims=False)
        send = lax.dynamic_index_in_dim(x, 1 - mine, axis, keepdims=False)
        return keep + swap_bit(send, *key), [k for k in left if k != key]

    left = names
    core, y_bit = ("ctx", 1), ("ctx", 2)
    z_bits = [("ctx", 1 << b) for b in range(2, ctx_bits)]
    f_bits = [("fsdp", 1 << b) for b in range(fsdp_bits)]
    x, left = halve(x, left, core)
    orders = [f_bits + [y_bit] + z_bits, [y_bit] + f_bits + z_bits, z_bits + f_bits + [y_bit]]
    cut = (cap * 2) // 5
    sizes = [cut, cut, cap - 2 * cut]
    parts, at = [], 0
    for order, size in zip(orders, sizes):
        piece = lax.slice_in_dim(x, at, at + size, axis=len(left))
        now = left
        for key in order:
            piece, now = halve(piece, now, key)
        parts.append(piece)
        at += size
    return jnp.concatenate(parts, axis=0)


def sum_all(x):
    for name in ("ctx", "fsdp"):
        for b in range(lax.axis_size(name).bit_length() - 1):
            x = x + swap_bit(x, name, 1 << b)
    return x


def scatter_kernel(counts, slot_ref, *refs):
    n = len(counts)
    grads, out, stage, sems = refs[:n], refs[n], refs[n + 1], refs[n + 2]
    lane = lax.broadcasted_iota(jnp.int32, (32, 128), 1) < 64
    base = 0
    for grad, (row_tiles, col_tiles) in zip(grads, counts):

        def drain(buf):
            pltpu.make_async_copy(
                stage.at[buf, pl.ds(0, col_tiles)], out.at[pl.ds(0, col_tiles)], sems.at[buf]
            ).wait()

        def strip(i, carry, grad=grad, base=base, col_tiles=col_tiles, drain=drain):
            buf = lax.rem(i, 2)

            @pl.when(i >= 2)
            def _():
                drain(buf)

            top = pl.ds(pl.multiple_of(i * 64, 64), 32)
            bottom = pl.ds(pl.multiple_of(i * 64 + 32, 32), 32)
            for j in range(col_tiles // 2):
                a = grad[top, j * 128 : (j + 1) * 128].astype(F32)
                b = grad[bottom, j * 128 : (j + 1) * 128].astype(F32)
                stage[buf, 2 * j] = jnp.where(lane, a, pltpu.roll(b, 64, 1)).astype(BF)
                stage[buf, 2 * j + 1] = jnp.where(lane, pltpu.roll(a, 64, 1), b).astype(BF)
            for j in range(col_tiles):
                slot = slot_ref[base + i * col_tiles + j]
                pltpu.make_async_copy(stage.at[buf, j], out.at[slot], sems.at[buf]).start()
            return carry

        lax.fori_loop(0, row_tiles, strip, 0)
        drain((row_tiles - 2) % 2)
        drain((row_tiles - 1) % 2)
        base += row_tiles * col_tiles


def scatter_tiles(grads, slot_table, slot_total):
    counts = tuple((g.shape[0] // 64, g.shape[1] // 64) for g in grads)
    widest = max(c for _, c in counts)
    return pl.pallas_call(
        functools.partial(scatter_kernel, counts),
        out_shape=jax.ShapeDtypeStruct((slot_total, 32, 128), BF),
        in_specs=[SM] + [VM] * len(grads),
        out_specs=pl.BlockSpec(memory_space=pl.ANY),
        scratch_shapes=[pltpu.VMEM((2, widest, 32, 128), BF), pltpu.SemaphoreType.DMA((2,))],
        compiler_params=pltpu.CompilerParams(vmem_limit_bytes=48 << 20),
        cost_estimate=pl.CostEstimate(flops=0, bytes_accessed=50 << 20, transcendentals=0),
        name="scatter_tiles",
    )(slot_table, *grads)


def soap_step(grads_in, weights_old, first_old, second_old, left_side, right_side):
    fine = lax.Precision.HIGH
    turned = jnp.einsum("bji,bjk->bik", left_side, grads_in, precision=fine)
    turned = jnp.einsum("bik,bkl->bil", turned, right_side, precision=fine)
    first_new = beta_one * first_old + (1.0 - beta_one) * turned
    second_new = beta_two * second_old + (1.0 - beta_two) * turned * turned
    normal_step = first_new / (jnp.sqrt(second_new) + adam_eps)
    restored = jnp.einsum("bij,bjk->bik", left_side, normal_step, precision=fine)
    restored = jnp.einsum("bik,blk->bil", restored, right_side, precision=fine)
    weights_new = weights_old - block_rate * (restored + decay_rate * weights_old)
    return (weights_new, first_new, second_new)


def gain_step(grads_in, gains_old, first_old, second_old):
    first_new = beta_one * first_old + (1.0 - beta_one) * grads_in
    second_new = beta_two * second_old + (1.0 - beta_two) * grads_in * grads_in
    gains_new = gains_old - gain_rate * first_new / (jnp.sqrt(second_new) + adam_eps)
    return (gains_new, first_new, second_new)


def on_device(
    inputs,
    cotangent,
    segments,
    w_qkv,
    w_out,
    w_in,
    w_down,
    norm_gains,
    slot_table,
    master,
    first_moment,
    rotated_second_moments,
    row_eigenbasis,
    column_eigenbasis,
    gain_master,
    gain_first,
    gain_second,
):
    micro, shard, width = inputs.shape
    heads = width // HEAD
    ctx_size = lax.axis_size("ctx")
    ctx_index = lax.axis_index("ctx")
    copies = max(1, ctx_size // heads)

    def spread(x):
        if copies > 1:
            x = jnp.repeat(x, copies, axis=0)
        return lax.all_to_all(x, "ctx", 0, 0, tiled=True)

    def collect(x):
        x = lax.all_to_all(x, "ctx", 0, 0, tiled=True)
        return x[::copies] if copies > 1 else x

    gains = lax.all_gather(norm_gains, "fsdp", axis=1, tiled=True).astype(F32)
    full_qkv = gather_rows(w_qkv)
    full_out = gather_rows(w_out)
    full_in = gather_rows(w_in)
    full_down = gather_rows(w_down)

    qkv_all, tables, normed_all, layer_ins = [], [], [], []
    for b in range(micro):
        seg_all = segments[b]
        cosine, sine = rope_tables(doc_positions(seg_all))
        tables.append((cosine, sine))
        own_cos = lax.dynamic_slice_in_dim(cosine, ctx_index * shard, shard, axis=1)
        own_sin = lax.dynamic_slice_in_dim(sine, ctx_index * shard, shard, axis=1)
        layer_in = inputs[b].astype(F32)
        normed = layer_norm(layer_in, gains[0]).astype(BF)
        proj = mm(full_qkv, normed, 0, 1).reshape(3, heads, HEAD, shard)

        def rotate(v, scale):
            a, c = v[:, : HEAD // 2], v[:, HEAD // 2 :]
            return jnp.concatenate([a * own_cos - c * own_sin, c * own_cos + a * own_sin], axis=1) * scale

        send = jnp.concatenate(
            [rotate(proj[0], LOG2E * HEAD**-0.5).astype(BF), rotate(proj[1], 1.0).astype(BF), proj[2].astype(BF)],
            axis=1,
        )
        qkv_all.append(spread(send))
        normed_all.append(normed)
        layer_ins.append(layer_in)

    attended_all, raw_all = [], []
    for b in range(micro):
        out, raw, lse = attend_forward(qkv_all[b], segments[b], bq=min(512, shard), bk=1024, sub=min(512, shard))
        raw_all.append((raw, lse))
        attended_all.append(collect(out).reshape(width, shard))

    outputs_list, d_middles, d_att_all = [], [], []
    hidden_all, d_gate_all, normed_two_all, branch_all = [], [], [], []
    gain_two_sum = 0.0
    for b in range(micro):
        middle_value = layer_ins[b] + mm(attended_all[b], full_out, 0, 0)
        normed_two = layer_norm(middle_value, gains[1]).astype(BF)
        gate_up = mm(normed_two, full_in, 1, 0)
        grad_top = cotangent[b]
        d_hidden = mm(grad_top, full_down, 1, 1)
        hidden, d_gate_up = gated_both(gate_up, d_hidden)
        hidden, d_gate_up = hidden.astype(BF), d_gate_up.astype(BF)
        result = middle_value + mm(hidden, full_down, 1, 0)
        outputs_list.append(result.astype(BF))
        d_normed_two = mm(d_gate_up, full_in, 1, 1)
        d_mid_norm, gain_two = norm_back(middle_value, gains[1], d_normed_two)
        d_middle = grad_top.astype(F32) + d_mid_norm
        grad_branch = d_middle.astype(BF)
        d_att = mm(full_out, grad_branch, 1, 1).astype(BF).reshape(heads, HEAD, shard)
        d_att_all.append(spread(d_att))
        d_middles.append(d_middle)
        hidden_all.append(hidden)
        d_gate_all.append(d_gate_up)
        normed_two_all.append(normed_two)
        branch_all.append(grad_branch)
        gain_two_sum = gain_two_sum + gain_two

    d_proj_all = []
    for b in range(micro):
        cosine, sine = tables[b]
        grads = attend_backward(
            qkv_all[b], segments[b], d_att_all[b], *raw_all[b], cosine, sine, bq=min(512, shard), bk=512, sub=256
        )
        d_proj_all.append(collect(grads))

    def rows(parts):
        return jnp.concatenate(parts, axis=0)

    grad_down = mm(rows(hidden_all), cotangent.reshape(-1, width), 0, 0).astype(BF)
    grad_in = mm(rows(normed_two_all), rows(d_gate_all), 0, 0).astype(BF)
    grad_out = mm(jnp.concatenate(attended_all, axis=1), rows(branch_all), 1, 0).astype(BF)

    d_proj = jnp.concatenate(d_proj_all, axis=2).reshape(heads, 3, HEAD, micro * shard)
    d_proj = d_proj.transpose(1, 0, 2, 3).reshape(3 * width, micro * shard)
    grad_qkv = mm(rows(normed_all), d_proj, 0, 1).astype(BF)
    slot_cap = master.shape[0]
    slot_total = slot_cap * ctx_size * lax.axis_size("fsdp")
    slotted = scatter_tiles([grad_qkv, grad_out, grad_in, grad_down], slot_table, slot_total)
    own_grads = reduce_parts(slotted)

    d_normed = mm(d_proj, full_qkv, 0, 1).reshape(micro, shard, width)
    input_grads = []
    gain_one_sum = 0.0
    for b in range(micro):
        d_in_norm, gain_one = norm_back(layer_ins[b], gains[0], d_normed[b])
        input_grads.append((d_middles[b] + d_in_norm).astype(BF))
        gain_one_sum = gain_one_sum + gain_one
    gain_grads = sum_all(jnp.stack([gain_one_sum, gain_two_sum]))

    device_index = lax.axis_index(("ctx", "fsdp"))
    own_ids = device_index * slot_cap + jnp.arange(slot_cap, dtype=jnp.int32)
    live_slot = jnp.any(slot_table[:, None] == own_ids[None, :], axis=0)[:, None, None]
    own_grads = own_grads.reshape(slot_cap, 32, 2, BLOCK_ORDER).transpose(0, 2, 1, 3)
    own_grads = own_grads.reshape(slot_cap, BLOCK_ORDER, BLOCK_ORDER).astype(F32)
    own_grads = jnp.where(live_slot, own_grads, 0.0)
    weights_new, first_new, second_new = soap_step(
        own_grads, master, first_moment, rotated_second_moments, row_eigenbasis, column_eigenbasis
    )
    new_master = jnp.where(live_slot, weights_new, master)
    new_first = jnp.where(live_slot, first_new, first_moment)
    new_second = jnp.where(live_slot, second_new, rotated_second_moments)
    new_gains, new_gain_first, new_gain_second = gain_step(gain_grads, gain_master, gain_first, gain_second)
    return (
        jnp.stack(outputs_list),
        jnp.stack(input_grads),
        own_grads,
        gain_grads,
        new_master,
        new_master.astype(BF),
        new_first,
        new_second,
        new_gains,
        new_gain_first,
        new_gain_second,
    )


def solution(mesh):
    tokens = P("fsdp", "ctx", None)
    slots = P(("ctx", "fsdp"), None, None)
    placed = (
        tokens,
        tokens,
        *(P("fsdp", None),) * 5,
        P(None, "fsdp"),
        P(),
        *(slots,) * 5,
        *(P(),) * 3,
    )
    return jax.shard_map(
        on_device,
        mesh=mesh,
        in_specs=placed,
        out_specs=(tokens, tokens, slots, P(), slots, slots, slots, slots, P(), P(), P()),
        check_vma=False,
    )
```

```python
import functools
import jax, jax.numpy as jnp
from jax import lax
from jax.experimental import pallas as pl
from jax.experimental.pallas import tpu as pltpu
from jax.sharding import PartitionSpec as P

HEAD = 64
NDOC=8
BIG=1e30
LN2=0.6931471805599453
LOG2E=1.4426950408889634

def split3(v):
    hi=v.astype(jnp.bfloat16)
    r=v-hi.astype(jnp.float32)
    mid=r.astype(jnp.bfloat16)
    lo=(r-mid.astype(jnp.float32)).astype(jnp.bfloat16)
    return hi.astype(jnp.float32),mid.astype(jnp.float32),lo.astype(jnp.float32)

def doc_rows(seg_row):
    n=seg_row.shape[1]
    ids=lax.broadcasted_iota(jnp.int32,(NDOC,n),0)
    return (ids==seg_row).astype(jnp.float32)

def fwd_kernel(bq,bk,sub,lo_ref,hi_ref,qkv_ref,seg_ref,out_ref,raw_ref,lse_ref,q_s,k_s,v_s):
    chunks,_,width=qkv_ref.shape
    full=chunks*width
    def prep(c,carry):
        cols=pl.ds(pl.multiple_of(c*width,width),width)
        hot=doc_rows(seg_ref[:,cols])
        zero8=jnp.zeros((8,width),jnp.float32)
        q_s[0:64,cols]=qkv_ref[c,0:64,:]
        q_s[64:80,cols]=jnp.concatenate([hot,zero8],0).astype(jnp.bfloat16)
        kt=jnp.concatenate([qkv_ref[c,64:128,:].astype(jnp.float32),(hot-1.0)*BIG,jnp.zeros((56,width),jnp.float32)],0)
        k_s[cols,:]=kt.T.astype(jnp.bfloat16)
        v_s[0:64,cols]=qkv_ref[c,128:192,:]
        row=lax.broadcasted_iota(jnp.int32,(16,width),0)
        v_s[64:80,cols]=(row==0).astype(jnp.bfloat16)
        return carry
    lax.fori_loop(0,chunks,prep,0)
    def q_step(i,carry):
        cols=pl.ds(pl.multiple_of(i*bq,bq),bq)
        qa=q_s[:,cols]
        def k_step(j,state):
            rows=pl.ds(pl.multiple_of(j*bk,bk),bk)
            ka=k_s[rows,0:80]
            va=v_s[:,rows]
            new=[]
            for n in range(bq//sub):
                m,acc=state[n]
                s=jnp.dot(ka,qa[:,n*sub:(n+1)*sub],preferred_element_type=jnp.float32)
                m_new=jnp.maximum(m,jnp.max(s,axis=0,keepdims=True))
                p=jnp.exp2(s-m_new).astype(jnp.bfloat16)
                acc=acc*jnp.exp2(m-m_new)+jnp.dot(va,p,preferred_element_type=jnp.float32)
                new.append((m_new,acc))
            return tuple(new)
        init=tuple((jnp.full((1,sub),-3e38,jnp.float32),jnp.zeros((80,sub),jnp.float32)) for _ in range(bq//sub))
        state=lax.fori_loop(lo_ref[i],hi_ref[i],k_step,init)
        m=jnp.concatenate([s[0] for s in state],1); acc=jnp.concatenate([s[1] for s in state],1)
        total=acc[64:65]
        o=acc[0:64]/total
        raw_ref[:,cols]=o
        lse_ref[:,cols]=m+jnp.log2(total)
        return carry
    lax.fori_loop(0,full//bq,q_step,0)
    def emit(c,carry):
        cols=pl.ds(pl.multiple_of(c*width,width),width)
        out_ref[c]=raw_ref[:,cols].astype(jnp.bfloat16)
        return carry
    lax.fori_loop(0,chunks,emit,0)

def bwd_kernel(bq,bk,sub,lo_ref,hi_ref,qkv_ref,seg_ref,do_ref,raw_ref,lse_ref,cos_ref,sin_ref,out_ref,flat_ref,
               q_s,kt_s,k_s,vt_s,do_s,qdt_s,dkv_s):
    chunks,_,width=qkv_ref.shape
    full=chunks*width
    def prep(c,carry):
        cols=pl.ds(pl.multiple_of(c*width,width),width)
        hot=doc_rows(seg_ref[:,cols])
        row=lax.broadcasted_iota(jnp.int32,(8,width),0)
        ones3=(row<3).astype(jnp.float32)
        def three(v):
            a,b,d=split3(-v)
            return jnp.where(row==0,a,jnp.where(row==1,b,jnp.where(row==2,d,0.0)))
        qt=qkv_ref[c,0:64,:]
        kt=qkv_ref[c,64:128,:]
        dt=do_ref[c]
        kt_s[0:64,cols]=kt
        kt_s[64:80,cols]=jnp.concatenate([(hot-1.0)*BIG,ones3],0).astype(jnp.bfloat16)
        vt_s[0:64,cols]=qkv_ref[c,128:192,:]
        vt_s[64:80,cols]=jnp.concatenate([ones3,jnp.zeros((8,width),jnp.float32)],0).astype(jnp.bfloat16)
        qdt_s[0:64,cols]=qt
        qdt_s[64:128,cols]=dt
        qq=jnp.concatenate([qt.astype(jnp.float32),hot,three(lse_ref[:,cols]),jnp.zeros((48,width),jnp.float32)],0)
        q_s[cols,:]=qq.T.astype(jnp.bfloat16)
        df=dt.astype(jnp.float32)
        delta=jnp.sum(df*raw_ref[:,cols],axis=0,keepdims=True)
        dd=jnp.concatenate([df,three(delta),jnp.zeros((56,width),jnp.float32)],0)
        do_s[cols,:]=dd.T.astype(jnp.bfloat16)
        kk=jnp.concatenate([kt.astype(jnp.float32),jnp.zeros((64,width),jnp.float32)],0)
        k_s[cols,:]=kk.T.astype(jnp.bfloat16)
        dkv_s[:,cols]=jnp.zeros((128,width),jnp.float32)
        return carry
    lax.fori_loop(0,chunks,prep,0)
    def q_step(i,carry):
        cols=pl.ds(pl.multiple_of(i*bq,bq),bq)
        qt=qdt_s[0:64,cols]; dt=qdt_s[64:128,cols]
        def k_step(j,dq):
            keys=pl.ds(pl.multiple_of(j*bk,bk),bk)
            dqs=[]; ps=[]; dss=[]
            for r in range(bq//sub):
                rr=pl.ds(pl.multiple_of(i*bq+r*sub,sub),sub)
                s=jnp.dot(q_s[rr,0:80],kt_s[:,keys],preferred_element_type=jnp.float32)
                dp=jnp.dot(do_s[rr,0:80],vt_s[:,keys],preferred_element_type=jnp.float32)
                p=jnp.exp2(s)
                ps.append(p.astype(jnp.bfloat16))
                ds=(p*dp).astype(jnp.bfloat16)
                dss.append(ds)
                dqs.append(jnp.dot(ds,k_s[keys,:],preferred_element_type=jnp.float32))
            ds=jnp.concatenate(dss,0); p16=jnp.concatenate(ps,0)
            dkv_s[0:64,keys]+=jnp.dot(qt,ds,preferred_element_type=jnp.float32)
            dkv_s[64:128,keys]+=jnp.dot(dt,p16,preferred_element_type=jnp.float32)
            return dq+jnp.concatenate(dqs,0)
        dq=lax.fori_loop(lo_ref[i],hi_ref[i],k_step,jnp.zeros((bq,128),jnp.float32))
        dq=(dq*0.125).T[0:64]
        c=cos_ref[:,cols]; s=sin_ref[:,cols]
        a,b=dq[0:32],dq[32:64]
        rot=jnp.concatenate([a*c+b*s,b*c-a*s],0).astype(jnp.bfloat16)
        flat_ref[0:64,cols]=rot
        return carry
    lax.fori_loop(0,full//bq,q_step,0)
    def emit(c,carry):
        cols=pl.ds(pl.multiple_of(c*width,width),width)
        t=dkv_s[:,cols]
        dk=t[0:64]*LN2
        co=cos_ref[:,cols]; si=sin_ref[:,cols]
        a,b=dk[0:32],dk[32:64]
        v=jnp.concatenate([a*co+b*si,b*co-a*si,t[64:128]],0).astype(jnp.bfloat16)
        flat_ref[64:192,cols]=v
        out_ref[c,0:64,:]=flat_ref[0:64,cols]
        out_ref[c,64:192,:]=v
        return carry
    lax.fori_loop(0,chunks,emit,0)

def ranges(seg_row,bq,bk):
    full=seg_row.shape[0]
    firsts=seg_row[::bq]; lasts=seg_row[bq-1::bq]
    lo=jnp.sum((seg_row[None,:]<firsts[:,None]).astype(jnp.int32),axis=1)//bk
    hi=-(-jnp.sum((seg_row[None,:]<=lasts[:,None]).astype(jnp.int32),axis=1)//bk)
    return lo.astype(jnp.int32),hi.astype(jnp.int32)

VM=pl.BlockSpec(memory_space=pltpu.VMEM)
SM=pl.BlockSpec(memory_space=pltpu.SMEM)
def attend_forward(qkv,seg_row,bq=512,bk=512,sub=256):
    chunks,_,width=qkv.shape; full=chunks*width
    lo,hi=ranges(seg_row,bq,bk)
    return pl.pallas_call(functools.partial(fwd_kernel,bq,bk,sub),
      out_shape=(jax.ShapeDtypeStruct((chunks,64,width),jnp.bfloat16),jax.ShapeDtypeStruct((64,full),jnp.float32),jax.ShapeDtypeStruct((1,full),jnp.float32)),
      in_specs=[SM,SM,VM,VM],out_specs=(VM,VM,VM),
      scratch_shapes=[pltpu.VMEM((80,full),jnp.bfloat16),pltpu.VMEM((full,128),jnp.bfloat16),pltpu.VMEM((80,full),jnp.bfloat16)],
      compiler_params=pltpu.CompilerParams(vmem_limit_bytes=40<<20),
      cost_estimate=pl.CostEstimate(flops=1140*full*full,bytes_accessed=8<<20,transcendentals=0),
      name="attend_fwd")(lo,hi,qkv,seg_row[None,:])
def attend_backward(qkv,seg_row,do,raw,lse,cos,sin,bq=512,bk=512,sub=512):
    chunks,_,width=qkv.shape; full=chunks*width
    lo,hi=ranges(seg_row,bq,bk)
    return pl.pallas_call(functools.partial(bwd_kernel,bq,bk,sub),
      out_shape=(jax.ShapeDtypeStruct((chunks,192,width),jnp.bfloat16),jax.ShapeDtypeStruct((192,full),jnp.bfloat16)),
      in_specs=[SM,SM,VM,VM,VM,VM,VM,VM,VM],out_specs=(VM,VM),
      scratch_shapes=[pltpu.VMEM((full,128),jnp.bfloat16),pltpu.VMEM((80,full),jnp.bfloat16),pltpu.VMEM((full,128),jnp.bfloat16),
        pltpu.VMEM((80,full),jnp.bfloat16),pltpu.VMEM((full,128),jnp.bfloat16),pltpu.VMEM((128,full),jnp.bfloat16),pltpu.VMEM((128,full),jnp.float32)],
      compiler_params=pltpu.CompilerParams(vmem_limit_bytes=56<<20),
      cost_estimate=pl.CostEstimate(flops=1580*full*full,bytes_accessed=16<<20,transcendentals=0),
      name="attend_bwd")(lo,hi,qkv,seg_row[None,:],do,raw,lse,cos,sin)

FF = 2624
BLOCK_ORDER = 64
rope_base = 160000.0
norm_eps = 1e-05
adam_eps = 1e-08
beta_one = 0.5
beta_two = 0.5
block_rate = 0.03
gain_rate = 0.75
decay_rate = 0.01
BF = jnp.bfloat16
F32 = jnp.float32


def layer_norm(values, gain_row):
    center = values - jnp.mean(values, axis=-1, keepdims=True)
    spread = jnp.mean(center * center, axis=-1, keepdims=True)
    return center * lax.rsqrt(spread + norm_eps) * gain_row


def norm_back(values, gain_row, grad_rows):
    unused, pullback = jax.vjp(layer_norm, values, gain_row)
    return pullback(grad_rows)


def doc_positions(seg_row):
    doc_ids = jnp.arange(NDOC, dtype=jnp.int32)
    matches = seg_row[:, None] == doc_ids[None, :]
    counts = jnp.sum(matches.astype(jnp.int32), axis=0)
    starts = jnp.cumsum(counts) - counts
    doc_begin = jnp.sum(jnp.where(matches, starts[None, :], 0), axis=1)
    return jnp.arange(seg_row.shape[0], dtype=jnp.int32) - doc_begin


def rope_tables(positions):
    half = HEAD // 2
    frequency = rope_base ** (-(jnp.arange(half, dtype=F32) * 2.0) / HEAD)
    angles = positions.astype(F32)[None, :] * frequency[:, None]
    return jnp.cos(angles), jnp.sin(angles)


def gated_gelu(gate_up):
    return jax.nn.gelu(gate_up[:, :FF], approximate=False) * gate_up[:, FF:]


def gated_both(gate_up, grad_hidden):
    hidden, pullback = jax.vjp(gated_gelu, gate_up)
    return hidden, pullback(grad_hidden)[0]


def mm(a, b, da, db):
    return lax.dot_general(a, b, (((da,), (db,)), ((), ())), preferred_element_type=F32)


def after(x, *others):
    return lax.optimization_barrier((x, *others))[0]


def swap_bit(x, axis, bit):
    n = lax.axis_size(axis)
    return lax.ppermute(x, axis, [(s, s ^ bit) for s in range(n)])


def two_parts():
    return lax.axis_size("fsdp") == 2 and lax.axis_size("ctx") % 2 == 0


def own_piece(shard):
    half = shard.shape[0] // 2
    return lax.dynamic_slice_in_dim(shard, (lax.axis_index("ctx") % 2) * half, half)


def joined(shard, got, twin):
    first = lax.axis_index("ctx") % 2 == 0
    mine = lax.axis_index("fsdp") == 0
    other = jnp.concatenate([jnp.where(first, got, twin), jnp.where(first, twin, got)], axis=0)
    return jnp.concatenate([jnp.where(mine, shard, other), jnp.where(mine, other, shard)], axis=0)


def halving_applies():
    return lax.axis_size("ctx") == 16 and lax.axis_size("fsdp") == 2


def half_of(x, axis, bit):
    return lax.dynamic_index_in_dim(x, bit, axis, keepdims=False)


def sum_all(x):
    for name in ("ctx", "fsdp"):
        for b in range(lax.axis_size(name).bit_length() - 1):
            x = x + swap_bit(x, name, 1 << b)
    return x


def scatter_kernel(counts, parts, where_ref, *refs):
    n = len(counts)
    grads, outs, stage, sems = refs[:n], refs[n : n + parts], refs[n + parts], refs[n + parts + 1]
    lane = lax.broadcasted_iota(jnp.int32, (32, 128), 1) < 64
    size = outs[0].shape[0]
    base = 0
    for grad, (row_tiles, col_tiles) in zip(grads, counts):

        def drain(buf):
            pltpu.make_async_copy(
                stage.at[buf, pl.ds(0, col_tiles)], outs[0].at[pl.ds(0, col_tiles)], sems.at[buf]
            ).wait()

        def strip(i, carry, grad=grad, base=base, col_tiles=col_tiles, drain=drain):
            buf = lax.rem(i, 2)

            @pl.when(i >= 2)
            def _():
                drain(buf)

            top = pl.ds(pl.multiple_of(i * 64, 64), 32)
            bottom = pl.ds(pl.multiple_of(i * 64 + 32, 32), 32)
            for j in range(col_tiles // 2):
                a = grad[top, j * 128 : (j + 1) * 128].astype(F32)
                b = grad[bottom, j * 128 : (j + 1) * 128].astype(F32)
                stage[buf, 2 * j] = jnp.where(lane, a, pltpu.roll(b, 64, 1)).astype(BF)
                stage[buf, 2 * j + 1] = jnp.where(lane, pltpu.roll(a, 64, 1), b).astype(BF)
            for j in range(col_tiles):
                place = where_ref[base + i * col_tiles + j]
                if parts == 1:
                    pltpu.make_async_copy(stage.at[buf, j], outs[0].at[place], sems.at[buf]).start()
                else:

                    @pl.when(place < size)
                    def _(j=j, place=place):
                        pltpu.make_async_copy(stage.at[buf, j], outs[0].at[place], sems.at[buf]).start()

                    @pl.when(place >= size)
                    def _(j=j, place=place):
                        pltpu.make_async_copy(stage.at[buf, j], outs[1].at[place - size], sems.at[buf]).start()

            return carry

        lax.fori_loop(0, row_tiles, strip, 0)
        drain((row_tiles - 2) % 2)
        drain((row_tiles - 1) % 2)
        base += row_tiles * col_tiles


def scatter_tiles(grads, where, total, parts):
    counts = tuple((g.shape[0] // 64, g.shape[1] // 64) for g in grads)
    widest = max(c for _, c in counts)
    return pl.pallas_call(
        functools.partial(scatter_kernel, counts, parts),
        out_shape=(jax.ShapeDtypeStruct((total // parts, 32, 128), BF),) * parts,
        in_specs=[SM] + [VM] * len(grads),
        out_specs=(pl.BlockSpec(memory_space=pl.ANY),) * parts,
        scratch_shapes=[pltpu.VMEM((2, widest, 32, 128), BF), pltpu.SemaphoreType.DMA((2,))],
        compiler_params=pltpu.CompilerParams(vmem_limit_bytes=48 << 20),
        cost_estimate=pl.CostEstimate(flops=40 << 30, bytes_accessed=40 << 20, transcendentals=0),
        name="scatter_tiles",
    )(where, *grads)


def soap_kernel(block, kind_ref, row_ref, col_ref, odd_ref, live_ref, qkv, early, master, first, second, left, right,
                grads_out, master_out, copy_out, first_out, second_out, tiles, sem):
    step = pl.program_id(0)
    total = tiles.shape[0]

    @pl.when(step == 0)
    def _():
        def fetch(n, carry):
            rows = pl.ds(pl.multiple_of(row_ref[n], 64), 64)
            cols = pl.ds(pl.multiple_of(col_ref[n], 128), 128)

            pltpu.make_async_copy(qkv.at[rows, cols], tiles.at[n], sem).start()
            return carry

        lax.fori_loop(0, total, fetch, 0)
        pltpu.make_async_copy(tiles, tiles, sem).wait()

    def two(v):
        hi = v.astype(BF)
        return hi, (v - hi.astype(F32)).astype(BF)

    def product(a, b):
        ah, al = two(a)
        bh, bl = two(b)
        return jnp.dot(
            jnp.concatenate([ah, ah, al], axis=1), jnp.concatenate([bh, bl, bh], axis=0), preferred_element_type=F32
        )

    def each(f, *lists):
        return [f(*row) for row in zip(*lists)]

    for low in range(0, block, 8):
        group = range(low, min(low + 8, block))

        def own_tile(k):
            n = jnp.minimum(step * block + k, total - 1)
            pair = tiles[n].astype(F32)
            turned = jnp.where(odd_ref[n] == 1, pair[:, 64:128], pair[:, 0:64]).T
            flat = early[k].astype(F32)
            tile = jnp.where(kind_ref[n] != 0, turned, jnp.concatenate([flat[:, 0:64], flat[:, 64:128]], axis=0))
            return jnp.where(live_ref[n] != 0, tile, 0.0)

        lives = [live_ref[jnp.minimum(step * block + k, total - 1)] != 0 for k in group]
        tile_list = [own_tile(k) for k in group]
        half = each(lambda k, t: product(left[k].T, t), group, tile_list)
        turned = each(lambda k, t: product(t, right[k]), group, half)
        firsts = each(lambda k, t: beta_one * first[k] + (1.0 - beta_one) * t, group, turned)
        seconds = each(lambda k, t: beta_two * second[k] + (1.0 - beta_two) * t * t, group, turned)
        normal = each(lambda f, s: f / (jnp.sqrt(s) + adam_eps), firsts, seconds)
        half = each(lambda k, t: product(left[k], t), group, normal)
        restored = each(lambda k, t: product(t, right[k].T), group, half)
        for k, live, tile, f, s, r in zip(group, lives, tile_list, firsts, seconds, restored):
            weights = master[k]
            new = jnp.where(live, weights - block_rate * (r + decay_rate * weights), weights)
            grads_out[k] = tile
            master_out[k] = new
            copy_out[k] = new.astype(BF)
            first_out[k] = jnp.where(live, f, first[k])
            second_out[k] = jnp.where(live, s, second[k])


def soap_step(picks, qkv, early, master, first, second, left, right):
    cap = master.shape[0]
    block = min(16, cap)
    spec = pl.BlockSpec((block, 64, 64), lambda i: (i, 0, 0))
    whole = pl.BlockSpec(memory_space=pl.ANY)
    like = jax.ShapeDtypeStruct(master.shape, F32)
    return pl.pallas_call(
        functools.partial(soap_kernel, block),
        grid=(-(-cap // block),),
        out_shape=(like, like, jax.ShapeDtypeStruct(master.shape, BF), like, like),
        in_specs=[SM] * 5 + [whole, pl.BlockSpec((block, 32, 128), lambda i: (i, 0, 0))] + [spec] * 5,
        out_specs=(spec,) * 5,
        scratch_shapes=[pltpu.VMEM((cap, 64, 128), BF), pltpu.SemaphoreType.DMA],
        compiler_params=pltpu.CompilerParams(vmem_limit_bytes=40 << 20),
        cost_estimate=pl.CostEstimate(flops=1 << 30, bytes_accessed=30 << 20, transcendentals=0),
        name="soap",
    )(*picks, qkv, early, master, first, second, left, right)


def own_picks(slot_table, slot_cap, heads):
    device_index = lax.axis_index(("ctx", "fsdp"))
    own_ids = device_index * slot_cap + jnp.arange(slot_cap, dtype=jnp.int32)
    hit = slot_table[None, :] == own_ids[:, None]
    live = jnp.any(hit, axis=1).astype(jnp.int32)
    tile = jnp.sum(jnp.where(hit, jnp.arange(slot_table.shape[0], dtype=jnp.int32)[None, :], 0), axis=1)
    across = heads * HEAD // 64
    is_qkv = tile < 3 * across * across
    q_row, q_col = tile // (3 * across), tile % (3 * across)
    row = jnp.where(is_qkv, (q_col % across) * 3 + q_col // across, 0)
    col = jnp.where(is_qkv, q_row, 0)
    return is_qkv.astype(jnp.int32), row * 64, (col // 2) * 128, col % 2, live


def gain_step(grads_in, gains_old, first_old, second_old):
    first_new = beta_one * first_old + (1.0 - beta_one) * grads_in
    second_new = beta_two * second_old + (1.0 - beta_two) * grads_in * grads_in
    gains_new = gains_old - gain_rate * first_new / (jnp.sqrt(second_new) + adam_eps)
    return (gains_new, first_new, second_new)


def on_device(
    inputs,
    cotangent,
    segments,
    w_qkv,
    w_out,
    w_in,
    w_down,
    norm_gains,
    slot_table,
    master,
    first_moment,
    rotated_second_moments,
    row_eigenbasis,
    column_eigenbasis,
    gain_master,
    gain_first,
    gain_second,
):
    micro, shard, width = inputs.shape
    heads = width // HEAD
    full_len = segments.shape[1]
    ctx_size = lax.axis_size("ctx")
    ctx_index = lax.axis_index("ctx")
    copies = max(1, ctx_size // heads)

    def spread(x):
        if copies > 1:
            x = jnp.repeat(x, copies, axis=0)
        return lax.all_to_all(x, "ctx", 0, 0, tiled=True)

    def collect(x):
        x = lax.all_to_all(x, "ctx", 0, 0, tiled=True)
        return x[::copies] if copies > 1 else x

    gains = lax.all_gather(norm_gains, "fsdp", axis=1, tiled=True).astype(F32)
    fast_gather = two_parts()
    if fast_gather:
        got_qkv = swap_bit(own_piece(w_qkv), "fsdp", 1)
        full_qkv = joined(w_qkv, got_qkv, swap_bit(got_qkv, "ctx", 1))
        later = [w_out, w_in, w_down]
        got_later = [swap_bit(after(own_piece(w), got_qkv), "fsdp", 1) for w in later]
    else:
        full_qkv, full_out, full_in, full_down = (
            lax.all_gather(w, "fsdp", axis=0, tiled=True) for w in (w_qkv, w_out, w_in, w_down)
        )

    qkv_all, tables, normed_all, layer_ins, sends = [], [], [], [], []
    for b in range(micro):
        seg_all = segments[b]
        positions = doc_positions(seg_all)
        tables.append(positions)
        own_cos, own_sin = rope_tables(lax.dynamic_slice_in_dim(positions, ctx_index * shard, shard))
        layer_in = inputs[b].astype(F32)
        normed = layer_norm(layer_in, gains[0]).astype(BF)
        proj = mm(full_qkv, normed, 0, 1).reshape(3, heads, HEAD, shard)

        def rotate(v, scale):
            a, c = v[:, : HEAD // 2], v[:, HEAD // 2 :]
            return jnp.concatenate([a * own_cos - c * own_sin, c * own_cos + a * own_sin], axis=1) * scale

        send = jnp.concatenate(
            [rotate(proj[0], LOG2E * HEAD**-0.5).astype(BF), rotate(proj[1], 1.0).astype(BF), proj[2].astype(BF)],
            axis=1,
        )
        sends.append(send)
        qkv_all.append(spread(send))
        normed_all.append(normed)
        layer_ins.append(layer_in)

    tables = [rope_tables(after(p, *sends)) for p in tables]
    attended_all, raw_all, outs = [], [], []
    for b in range(micro):
        ready = after(qkv_all[b], *(outs[-1:] or sends))
        out, raw, lse = attend_forward(ready, segments[b], bq=min(1024, full_len), bk=512, sub=min(1024, full_len))
        outs.append(out)
        raw_all.append((raw, lse))
        attended_all.append(collect(out).reshape(width, shard))
    wide = lax.all_gather(after(jnp.stack(normed_all), qkv_all[-1]), "ctx", axis=1, tiled=True)
    normed_wide = [wide[b] for b in range(micro)]
    if fast_gather:
        got_later = [after(g, outs[0]) for g in got_later]
        twins = [after(swap_bit(g, "ctx", 1), outs[-1]) for g in got_later]
        full_out, full_in, full_down = (joined(*parts) for parts in zip(later, got_later, twins))

    outputs_list, d_middles, d_att_all = [], [], []
    hidden_all, d_gate_all, normed_two_all, branch_all = [], [], [], []
    gain_two_sum = 0.0
    for b in range(micro):
        if b:
            attended_all[b] = after(attended_all[b], branch_all[b - 1])
        middle_value = layer_ins[b] + mm(attended_all[b], full_out, 0, 0)
        normed_two = layer_norm(middle_value, gains[1]).astype(BF)
        gate_up = mm(normed_two, full_in, 1, 0)
        grad_top = cotangent[b]
        d_hidden = mm(grad_top, full_down, 1, 1)
        hidden, d_gate_up = gated_both(gate_up, d_hidden)
        hidden, d_gate_up = hidden.astype(BF), d_gate_up.astype(BF)
        result = middle_value + mm(hidden, full_down, 1, 0)
        outputs_list.append(result.astype(BF))
        d_normed_two = mm(d_gate_up, full_in, 1, 1)
        d_mid_norm, gain_two = norm_back(middle_value, gains[1], d_normed_two)
        d_middle = grad_top.astype(F32) + d_mid_norm
        grad_branch = d_middle.astype(BF)
        d_att = mm(full_out, grad_branch, 1, 1).astype(BF).reshape(heads, HEAD, shard)
        d_att_all.append(spread(d_att))
        d_middles.append(d_middle)
        hidden_all.append(hidden)
        d_gate_all.append(d_gate_up)
        normed_two_all.append(normed_two)
        branch_all.append(grad_branch)
        gain_two_sum = gain_two_sum + gain_two

    def rows(parts):
        return jnp.concatenate(parts, axis=0)

    grad_out = mm(jnp.concatenate(attended_all, axis=1), rows(branch_all), 1, 0).astype(BF)
    grad_in = mm(rows(normed_two_all), rows(d_gate_all), 0, 0).astype(BF)
    grad_down = mm(rows(hidden_all), cotangent.reshape(-1, width), 0, 0).astype(BF)
    slot_cap = master.shape[0]
    slot_total = slot_cap * ctx_size * lax.axis_size("fsdp")
    where = after(slot_table[3 * (width // 64) ** 2 :], d_att_all[0])
    fast = halving_applies() and micro == 2
    waits = [()] * micro
    if fast:
        owner = where // slot_cap
        rest = where % slot_cap
        cut = slot_cap // 2
        low = rest < cut
        core = (owner // 2) % 2
        x_rel = (owner % 2) ^ lax.axis_index("fsdp")
        ctx_rel = (owner // 2) ^ ctx_index
        y_rel, z_one, z_two = (ctx_rel // 2) % 2, (ctx_rel // 4) % 2, ctx_rel // 8
        z_rel = z_one * 2 + z_two
        place = jnp.where(
            low,
            ((x_rel * 2 + y_rel) * 4 + z_rel) * cut + rest,
            16 * cut + ((y_rel * 2 + x_rel) * 4 + z_rel) * (slot_cap - cut) + rest - cut,
        )
        where = place + jnp.where(core == ctx_index % 2, slot_total // 2, 0)
        send, keep = scatter_tiles([grad_out, grad_in, grad_down], where, slot_total, 2)
        got = swap_bit(send, "ctx", 1)

        def both(low, high):
            return keep[low:high] + got[low:high]

        ours = [both(0, 8 * cut), both(16 * cut, 16 * cut + 8 * (slot_cap - cut))]
        theirs = [both(8 * cut, 16 * cut), both(16 * cut + 8 * (slot_cap - cut), 16 * slot_cap)]
        near = [swap_bit(theirs[0], "fsdp", 1), swap_bit(theirs[1], "ctx", 2)]
        waits[0] = (*ours, *theirs)
    else:
        (slotted,) = scatter_tiles([grad_out, grad_in, grad_down], where, slot_total, 1)
        own_slots = lax.psum_scatter(slotted, ("ctx", "fsdp"), scatter_dimension=0, tiled=True)

    d_proj_all, grad_heads = [], 0.0
    for b in range(micro):
        cosine, sine = tables[b]
        d_att = after(d_att_all[b], *waits[b])
        grads, flat = attend_backward(
            qkv_all[b], segments[b], d_att, *raw_all[b], cosine, sine, bq=512, bk=512, sub=512
        )
        if fast and b == 0:
            near = [after(v, grads) for v in near]
            next_ours = [t[: t.shape[0] // 2] + v[: t.shape[0] // 2] for t, v in zip(ours, near)]
            next_theirs = [t[t.shape[0] // 2 :] + v[t.shape[0] // 2 :] for t, v in zip(ours, near)]
            next_near = [swap_bit(next_theirs[0], "ctx", 2), swap_bit(next_theirs[1], "fsdp", 1)]
            waits[1] = (*next_ours, *next_theirs)
        elif fast:
            next_near = [after(v, grads) for v in next_near]
            pair = [(t.reshape(2, 2, -1, 32, 128), v.reshape(2, 2, -1, 32, 128)) for t, v in zip(next_ours, next_near)]
            kept, sent = (jnp.concatenate([t[side] + v[side] for t, v in pair], axis=1) for side in (0, 1))
            got = swap_bit(sent, "ctx", 4)
            kept, sent = (kept[side] + got[side] for side in (0, 1))
            own_slots = kept + swap_bit(sent, "ctx", 8)
        d_proj_all.append(collect(grads))
        grad_heads = grad_heads + mm(flat, normed_wide[b], 1, 0)

    grad_heads = after(grad_heads.astype(BF), d_proj_all[0], *(next_near if fast else ()))
    if lax.axis_size("fsdp") == 2:
        grad_heads = grad_heads + swap_bit(grad_heads, "fsdp", 1)
    else:
        grad_heads = lax.psum(grad_heads, "fsdp")
    grad_qkv = lax.all_gather(grad_heads[None], "ctx", axis=0, tiled=True)[::copies].reshape(3 * width, width)

    input_grads = []
    gain_one_sum = 0.0
    for b in range(micro):
        d_proj = d_proj_all[b].reshape(heads, 3, HEAD, shard).transpose(1, 0, 2, 3).reshape(3 * width, shard)
        d_normed = mm(d_proj, full_qkv, 0, 1)
        d_in_norm, gain_one = norm_back(layer_ins[b], gains[0], d_normed)
        input_grads.append((d_middles[b] + d_in_norm).astype(BF))
        gain_one_sum = gain_one_sum + gain_one
    gain_grads = sum_all(jnp.stack([gain_one_sum, gain_two_sum]))

    picks = own_picks(slot_table, slot_cap, heads)
    own_grads, new_master, new_copy, new_first, new_second = soap_step(
        picks, grad_qkv, own_slots, master, first_moment, rotated_second_moments, row_eigenbasis, column_eigenbasis
    )
    new_gains, new_gain_first, new_gain_second = gain_step(gain_grads, gain_master, gain_first, gain_second)
    return (
        jnp.stack(outputs_list),
        jnp.stack(input_grads),
        own_grads,
        gain_grads,
        new_master,
        new_copy,
        new_first,
        new_second,
        new_gains,
        new_gain_first,
        new_gain_second,
    )


def solution(mesh):
    tokens = P("fsdp", "ctx", None)
    slots = P(("ctx", "fsdp"), None, None)
    placed = (
        tokens,
        tokens,
        *(P("fsdp", None),) * 5,
        P(None, "fsdp"),
        P(),
        *(slots,) * 5,
        *(P(),) * 3,
    )
    return jax.shard_map(
        on_device,
        mesh=mesh,
        in_specs=placed,
        out_specs=(tokens, tokens, slots, P(), slots, slots, slots, slots, P(), P(), P()),
        check_vma=False,
    )
```

```python
import functools
import jax, jax.numpy as jnp
from jax import lax
from jax.experimental import pallas as pl
from jax.experimental.pallas import tpu as pltpu
from jax.sharding import PartitionSpec as P

HEAD = 64
NDOC=8
BIG=1e30
LN2=0.6931471805599453
LOG2E=1.4426950408889634

def split3(v):
    hi=v.astype(jnp.bfloat16)
    r=v-hi.astype(jnp.float32)
    mid=r.astype(jnp.bfloat16)
    lo=(r-mid.astype(jnp.float32)).astype(jnp.bfloat16)
    return hi.astype(jnp.float32),mid.astype(jnp.float32),lo.astype(jnp.float32)

def doc_rows(seg_row):
    n=seg_row.shape[1]
    ids=lax.broadcasted_iota(jnp.int32,(NDOC,n),0)
    return (ids==seg_row).astype(jnp.float32)

def fwd_kernel(bq,bk,sub,lo_ref,hi_ref,qkv_ref,seg_ref,out_ref,raw_ref,lse_ref,q_s,k_s,v_s):
    chunks,_,width=qkv_ref.shape
    full=chunks*width
    def prep(c,carry):
        cols=pl.ds(pl.multiple_of(c*width,width),width)
        hot=doc_rows(seg_ref[:,cols])
        zero8=jnp.zeros((8,width),jnp.float32)
        q_s[0:64,cols]=qkv_ref[c,0:64,:]
        q_s[64:80,cols]=jnp.concatenate([hot,zero8],0).astype(jnp.bfloat16)
        kt=jnp.concatenate([qkv_ref[c,64:128,:].astype(jnp.float32),(hot-1.0)*BIG,jnp.zeros((56,width),jnp.float32)],0)
        k_s[cols,:]=kt.T.astype(jnp.bfloat16)
        v_s[0:64,cols]=qkv_ref[c,128:192,:]
        row=lax.broadcasted_iota(jnp.int32,(16,width),0)
        v_s[64:80,cols]=(row==0).astype(jnp.bfloat16)
        return carry
    lax.fori_loop(0,chunks,prep,0)
    def q_step(i,carry):
        cols=pl.ds(pl.multiple_of(i*bq,bq),bq)
        qa=q_s[:,cols]
        def k_step(j,state):
            rows=pl.ds(pl.multiple_of(j*bk,bk),bk)
            ka=k_s[rows,0:80]
            va=v_s[:,rows]
            new=[]
            for n in range(bq//sub):
                m,acc=state[n]
                s=jnp.dot(ka,qa[:,n*sub:(n+1)*sub],preferred_element_type=jnp.float32)
                m_new=jnp.maximum(m,jnp.max(s,axis=0,keepdims=True))
                p=jnp.exp2(s-m_new).astype(jnp.bfloat16)
                acc=acc*jnp.exp2(m-m_new)+jnp.dot(va,p,preferred_element_type=jnp.float32)
                new.append((m_new,acc))
            return tuple(new)
        init=tuple((jnp.full((1,sub),-3e38,jnp.float32),jnp.zeros((80,sub),jnp.float32)) for _ in range(bq//sub))
        state=lax.fori_loop(lo_ref[i],hi_ref[i],k_step,init)
        m=jnp.concatenate([s[0] for s in state],1); acc=jnp.concatenate([s[1] for s in state],1)
        total=acc[64:65]
        o=acc[0:64]/total
        raw_ref[:,cols]=o
        lse_ref[:,cols]=m+jnp.log2(total)
        return carry
    lax.fori_loop(0,full//bq,q_step,0)
    def emit(c,carry):
        cols=pl.ds(pl.multiple_of(c*width,width),width)
        out_ref[c]=raw_ref[:,cols].astype(jnp.bfloat16)
        return carry
    lax.fori_loop(0,chunks,emit,0)

def bwd_kernel(bq,bk,sub,lo_ref,hi_ref,qkv_ref,seg_ref,do_ref,raw_ref,lse_ref,cos_ref,sin_ref,out_ref,flat_ref,
               q_s,kt_s,k_s,vt_s,do_s,qdt_s,dkv_s):
    chunks,_,width=qkv_ref.shape
    full=chunks*width
    def prep(c,carry):
        cols=pl.ds(pl.multiple_of(c*width,width),width)
        hot=doc_rows(seg_ref[:,cols])
        row=lax.broadcasted_iota(jnp.int32,(8,width),0)
        ones3=(row<3).astype(jnp.float32)
        def three(v):
            a,b,d=split3(-v)
            return jnp.where(row==0,a,jnp.where(row==1,b,jnp.where(row==2,d,0.0)))
        qt=qkv_ref[c,0:64,:]
        kt=qkv_ref[c,64:128,:]
        dt=do_ref[c]
        kt_s[0:64,cols]=kt
        kt_s[64:80,cols]=jnp.concatenate([(hot-1.0)*BIG,ones3],0).astype(jnp.bfloat16)
        vt_s[0:64,cols]=qkv_ref[c,128:192,:]
        vt_s[64:80,cols]=jnp.concatenate([ones3,jnp.zeros((8,width),jnp.float32)],0).astype(jnp.bfloat16)
        qdt_s[0:64,cols]=qt
        qdt_s[64:128,cols]=dt
        qq=jnp.concatenate([qt.astype(jnp.float32),hot,three(lse_ref[:,cols]),jnp.zeros((48,width),jnp.float32)],0)
        q_s[cols,:]=qq.T.astype(jnp.bfloat16)
        df=dt.astype(jnp.float32)
        delta=jnp.sum(df*raw_ref[:,cols],axis=0,keepdims=True)
        dd=jnp.concatenate([df,three(delta),jnp.zeros((56,width),jnp.float32)],0)
        do_s[cols,:]=dd.T.astype(jnp.bfloat16)
        kk=jnp.concatenate([kt.astype(jnp.float32),jnp.zeros((64,width),jnp.float32)],0)
        k_s[cols,:]=kk.T.astype(jnp.bfloat16)
        dkv_s[:,cols]=jnp.zeros((128,width),jnp.float32)
        return carry
    lax.fori_loop(0,chunks,prep,0)
    def q_step(i,carry):
        cols=pl.ds(pl.multiple_of(i*bq,bq),bq)
        qt=qdt_s[0:64,cols]; dt=qdt_s[64:128,cols]
        def k_step(j,dq):
            keys=pl.ds(pl.multiple_of(j*bk,bk),bk)
            dqs=[]; ps=[]; dss=[]
            for r in range(bq//sub):
                rr=pl.ds(pl.multiple_of(i*bq+r*sub,sub),sub)
                s=jnp.dot(q_s[rr,0:80],kt_s[:,keys],preferred_element_type=jnp.float32)
                dp=jnp.dot(do_s[rr,0:80],vt_s[:,keys],preferred_element_type=jnp.float32)
                p=jnp.exp2(s)
                ps.append(p.astype(jnp.bfloat16))
                ds=(p*dp).astype(jnp.bfloat16)
                dss.append(ds)
                dqs.append(jnp.dot(ds,k_s[keys,:],preferred_element_type=jnp.float32))
            ds=jnp.concatenate(dss,0); p16=jnp.concatenate(ps,0)
            dkv_s[0:64,keys]+=jnp.dot(qt,ds,preferred_element_type=jnp.float32)
            dkv_s[64:128,keys]+=jnp.dot(dt,p16,preferred_element_type=jnp.float32)
            return dq+jnp.concatenate(dqs,0)
        dq=lax.fori_loop(lo_ref[i],hi_ref[i],k_step,jnp.zeros((bq,128),jnp.float32))
        dq=(dq*0.125).T[0:64]
        c=cos_ref[:,cols]; s=sin_ref[:,cols]
        a,b=dq[0:32],dq[32:64]
        rot=jnp.concatenate([a*c+b*s,b*c-a*s],0).astype(jnp.bfloat16)
        flat_ref[0:64,cols]=rot
        return carry
    lax.fori_loop(0,full//bq,q_step,0)
    def emit(c,carry):
        cols=pl.ds(pl.multiple_of(c*width,width),width)
        t=dkv_s[:,cols]
        dk=t[0:64]*LN2
        co=cos_ref[:,cols]; si=sin_ref[:,cols]
        a,b=dk[0:32],dk[32:64]
        v=jnp.concatenate([a*co+b*si,b*co-a*si,t[64:128]],0).astype(jnp.bfloat16)
        flat_ref[64:192,cols]=v
        out_ref[c,0:64,:]=flat_ref[0:64,cols]
        out_ref[c,64:192,:]=v
        return carry
    lax.fori_loop(0,chunks,emit,0)

def ranges(seg_row,bq,bk):
    full=seg_row.shape[0]
    firsts=seg_row[::bq]; lasts=seg_row[bq-1::bq]
    lo=jnp.sum((seg_row[None,:]<firsts[:,None]).astype(jnp.int32),axis=1)//bk
    hi=-(-jnp.sum((seg_row[None,:]<=lasts[:,None]).astype(jnp.int32),axis=1)//bk)
    return lo.astype(jnp.int32),hi.astype(jnp.int32)

VM=pl.BlockSpec(memory_space=pltpu.VMEM)
SM=pl.BlockSpec(memory_space=pltpu.SMEM)
def attend_forward(qkv,seg_row,bq=512,bk=512,sub=256):
    chunks,_,width=qkv.shape; full=chunks*width
    lo,hi=ranges(seg_row,bq,bk)
    return pl.pallas_call(functools.partial(fwd_kernel,bq,bk,sub),
      out_shape=(jax.ShapeDtypeStruct((chunks,64,width),jnp.bfloat16),jax.ShapeDtypeStruct((64,full),jnp.float32),jax.ShapeDtypeStruct((1,full),jnp.float32)),
      in_specs=[SM,SM,VM,VM],out_specs=(VM,VM,VM),
      scratch_shapes=[pltpu.VMEM((80,full),jnp.bfloat16),pltpu.VMEM((full,128),jnp.bfloat16),pltpu.VMEM((80,full),jnp.bfloat16)],
      compiler_params=pltpu.CompilerParams(vmem_limit_bytes=40<<20),
      cost_estimate=pl.CostEstimate(flops=1140*full*full,bytes_accessed=8<<20,transcendentals=0),
      name="attend_fwd")(lo,hi,qkv,seg_row[None,:])
def attend_backward(qkv,seg_row,do,raw,lse,cos,sin,bq=512,bk=512,sub=512):
    chunks,_,width=qkv.shape; full=chunks*width
    lo,hi=ranges(seg_row,bq,bk)
    return pl.pallas_call(functools.partial(bwd_kernel,bq,bk,sub),
      out_shape=(jax.ShapeDtypeStruct((chunks,192,width),jnp.bfloat16),jax.ShapeDtypeStruct((192,full),jnp.bfloat16)),
      in_specs=[SM,SM,VM,VM,VM,VM,VM,VM,VM],out_specs=(VM,VM),
      scratch_shapes=[pltpu.VMEM((full,128),jnp.bfloat16),pltpu.VMEM((80,full),jnp.bfloat16),pltpu.VMEM((full,128),jnp.bfloat16),
        pltpu.VMEM((80,full),jnp.bfloat16),pltpu.VMEM((full,128),jnp.bfloat16),pltpu.VMEM((128,full),jnp.bfloat16),pltpu.VMEM((128,full),jnp.float32)],
      compiler_params=pltpu.CompilerParams(vmem_limit_bytes=56<<20),
      cost_estimate=pl.CostEstimate(flops=1580*full*full,bytes_accessed=16<<20,transcendentals=0),
      name="attend_bwd")(lo,hi,qkv,seg_row[None,:],do,raw,lse,cos,sin)

FF = 2624
BLOCK_ORDER = 64
rope_base = 160000.0
norm_eps = 1e-05
adam_eps = 1e-08
beta_one = 0.5
beta_two = 0.5
block_rate = 0.03
gain_rate = 0.75
decay_rate = 0.01
BF = jnp.bfloat16
F32 = jnp.float32


def layer_norm(values, gain_row):
    center = values - jnp.mean(values, axis=-1, keepdims=True)
    spread = jnp.mean(center * center, axis=-1, keepdims=True)
    return center * lax.rsqrt(spread + norm_eps) * gain_row


def norm_back(values, gain_row, grad_rows):
    unused, pullback = jax.vjp(layer_norm, values, gain_row)
    return pullback(grad_rows)


def doc_positions(seg_row):
    doc_ids = jnp.arange(NDOC, dtype=jnp.int32)
    matches = seg_row[:, None] == doc_ids[None, :]
    counts = jnp.sum(matches.astype(jnp.int32), axis=0)
    starts = jnp.cumsum(counts) - counts
    doc_begin = jnp.sum(jnp.where(matches, starts[None, :], 0), axis=1)
    return jnp.arange(seg_row.shape[0], dtype=jnp.int32) - doc_begin


def rope_tables(positions):
    half = HEAD // 2
    frequency = rope_base ** (-(jnp.arange(half, dtype=F32) * 2.0) / HEAD)
    angles = positions.astype(F32)[None, :] * frequency[:, None]
    return jnp.cos(angles), jnp.sin(angles)


def gated_gelu(gate_up):
    return jax.nn.gelu(gate_up[:, :FF], approximate=False) * gate_up[:, FF:]


def gated_both(gate_up, grad_hidden):
    hidden, pullback = jax.vjp(gated_gelu, gate_up)
    return hidden, pullback(grad_hidden)[0]


def mm(a, b, da, db):
    return lax.dot_general(a, b, (((da,), (db,)), ((), ())), preferred_element_type=F32)


def after(x, *others):
    return lax.optimization_barrier((x, *others))[0]


def swap_bit(x, axis, bit):
    n = lax.axis_size(axis)
    return lax.ppermute(x, axis, [(s, s ^ bit) for s in range(n)])


def two_parts():
    return lax.axis_size("fsdp") == 2 and lax.axis_size("ctx") % 2 == 0


def own_piece(shard):
    half = shard.shape[0] // 2
    return lax.dynamic_slice_in_dim(shard, (lax.axis_index("ctx") % 2) * half, half)


def joined(shard, got, twin):
    first = lax.axis_index("ctx") % 2 == 0
    mine = lax.axis_index("fsdp") == 0
    other = jnp.concatenate([jnp.where(first, got, twin), jnp.where(first, twin, got)], axis=0)
    return jnp.concatenate([jnp.where(mine, shard, other), jnp.where(mine, other, shard)], axis=0)


def halving_applies():
    return lax.axis_size("ctx") == 16 and lax.axis_size("fsdp") == 2


def half_of(x, axis, bit):
    return lax.dynamic_index_in_dim(x, bit, axis, keepdims=False)


def sum_all(x):
    for name in ("ctx", "fsdp"):
        for b in range(lax.axis_size(name).bit_length() - 1):
            x = x + swap_bit(x, name, 1 << b)
    return x


def scatter_kernel(counts, parts, where_ref, *refs):
    n = len(counts)
    grads, outs, stage, sems = refs[:n], refs[n : n + parts], refs[n + parts], refs[n + parts + 1]
    lane = lax.broadcasted_iota(jnp.int32, (32, 128), 1) < 64
    size = outs[0].shape[0]
    base = 0
    for grad, (row_tiles, col_tiles) in zip(grads, counts):

        def drain(buf):
            pltpu.make_async_copy(
                stage.at[buf, pl.ds(0, col_tiles)], outs[0].at[pl.ds(0, col_tiles)], sems.at[buf]
            ).wait()

        def strip(i, carry, grad=grad, base=base, col_tiles=col_tiles, drain=drain):
            buf = lax.rem(i, 2)

            @pl.when(i >= 2)
            def _():
                drain(buf)

            top = pl.ds(pl.multiple_of(i * 64, 64), 32)
            bottom = pl.ds(pl.multiple_of(i * 64 + 32, 32), 32)
            for j in range(col_tiles // 2):
                a = grad[top, j * 128 : (j + 1) * 128].astype(F32)
                b = grad[bottom, j * 128 : (j + 1) * 128].astype(F32)
                stage[buf, 2 * j] = jnp.where(lane, a, pltpu.roll(b, 64, 1)).astype(BF)
                stage[buf, 2 * j + 1] = jnp.where(lane, pltpu.roll(a, 64, 1), b).astype(BF)
            for j in range(col_tiles):
                place = where_ref[base + i * col_tiles + j]
                if parts == 1:
                    pltpu.make_async_copy(stage.at[buf, j], outs[0].at[place], sems.at[buf]).start()
                else:

                    @pl.when(place < size)
                    def _(j=j, place=place):
                        pltpu.make_async_copy(stage.at[buf, j], outs[0].at[place], sems.at[buf]).start()

                    @pl.when(place >= size)
                    def _(j=j, place=place):
                        pltpu.make_async_copy(stage.at[buf, j], outs[1].at[place - size], sems.at[buf]).start()

            return carry

        lax.fori_loop(0, row_tiles, strip, 0)
        drain((row_tiles - 2) % 2)
        drain((row_tiles - 1) % 2)
        base += row_tiles * col_tiles


def scatter_tiles(grads, where, total, parts):
    counts = tuple((g.shape[0] // 64, g.shape[1] // 64) for g in grads)
    widest = max(c for _, c in counts)
    return pl.pallas_call(
        functools.partial(scatter_kernel, counts, parts),
        out_shape=(jax.ShapeDtypeStruct((total // parts, 32, 128), BF),) * parts,
        in_specs=[SM] + [VM] * len(grads),
        out_specs=(pl.BlockSpec(memory_space=pl.ANY),) * parts,
        scratch_shapes=[pltpu.VMEM((2, widest, 32, 128), BF), pltpu.SemaphoreType.DMA((2,))],
        compiler_params=pltpu.CompilerParams(vmem_limit_bytes=48 << 20),
        cost_estimate=pl.CostEstimate(flops=40 << 30, bytes_accessed=40 << 20, transcendentals=0),
        name="scatter_tiles",
    )(where, *grads)


def soap_kernel(block, kind_ref, pick_ref, live_ref, pool, early, master, first, second, left, right,
                grads_out, master_out, copy_out, first_out, second_out, tiles, sem):
    step = pl.program_id(0)
    total = tiles.shape[0]

    @pl.when(step == 0)
    def _():
        def fetch(n, carry):
            pltpu.make_async_copy(pool.at[pick_ref[n]], tiles.at[n], sem).start()
            return carry

        lax.fori_loop(0, total, fetch, 0)
        pltpu.make_async_copy(tiles, tiles, sem).wait()

    def two(v):
        hi = v.astype(BF)
        return hi, (v - hi.astype(F32)).astype(BF)

    def product(a, b):
        ah, al = two(a)
        bh, bl = two(b)
        return jnp.dot(
            jnp.concatenate([ah, ah, al], axis=1), jnp.concatenate([bh, bl, bh], axis=0), preferred_element_type=F32
        )

    def each(f, *lists):
        return [f(*row) for row in zip(*lists)]

    for low in range(0, block, 8):
        group = range(low, min(low + 8, block))

        def own_tile(k):
            n = jnp.minimum(step * block + k, total - 1)
            flat = jnp.where(kind_ref[n] != 0, tiles[n].astype(F32), early[k].astype(F32))
            tile = jnp.concatenate([flat[:, 0:64], flat[:, 64:128]], axis=0)
            return jnp.where(live_ref[n] != 0, tile, 0.0)

        lives = [live_ref[jnp.minimum(step * block + k, total - 1)] != 0 for k in group]
        tile_list = [own_tile(k) for k in group]
        half = each(lambda k, t: product(left[k].T, t), group, tile_list)
        turned = each(lambda k, t: product(t, right[k]), group, half)
        firsts = each(lambda k, t: beta_one * first[k] + (1.0 - beta_one) * t, group, turned)
        seconds = each(lambda k, t: beta_two * second[k] + (1.0 - beta_two) * t * t, group, turned)
        normal = each(lambda f, s: f / (jnp.sqrt(s) + adam_eps), firsts, seconds)
        half = each(lambda k, t: product(left[k], t), group, normal)
        restored = each(lambda k, t: product(t, right[k].T), group, half)
        for k, live, tile, f, s, r in zip(group, lives, tile_list, firsts, seconds, restored):
            weights = master[k]
            new = jnp.where(live, weights - block_rate * (r + decay_rate * weights), weights)
            grads_out[k] = tile
            master_out[k] = new
            copy_out[k] = new.astype(BF)
            first_out[k] = jnp.where(live, f, first[k])
            second_out[k] = jnp.where(live, s, second[k])


def soap_step(picks, pool, early, master, first, second, left, right):
    cap = master.shape[0]
    block = min(16, cap)
    spec = pl.BlockSpec((block, 64, 64), lambda i: (i, 0, 0))
    whole = pl.BlockSpec(memory_space=pl.ANY)
    like = jax.ShapeDtypeStruct(master.shape, F32)
    return pl.pallas_call(
        functools.partial(soap_kernel, block),
        grid=(-(-cap // block),),
        out_shape=(like, like, jax.ShapeDtypeStruct(master.shape, BF), like, like),
        in_specs=[SM] * 3 + [whole, pl.BlockSpec((block, 32, 128), lambda i: (i, 0, 0))] + [spec] * 5,
        out_specs=(spec,) * 5,
        scratch_shapes=[pltpu.VMEM((cap, 32, 128), BF), pltpu.SemaphoreType.DMA],
        compiler_params=pltpu.CompilerParams(vmem_limit_bytes=40 << 20),
        cost_estimate=pl.CostEstimate(flops=23 << 30, bytes_accessed=30 << 20, transcendentals=0),
        name="soap",
    )(*picks, pool, early, master, first, second, left, right)


def own_tiles(slot_table, slot_cap):
    device_index = lax.axis_index(("ctx", "fsdp"))
    own_ids = device_index * slot_cap + jnp.arange(slot_cap, dtype=jnp.int32)
    hit = slot_table[None, :] == own_ids[:, None]
    live = jnp.any(hit, axis=1).astype(jnp.int32)
    tile = jnp.sum(jnp.where(hit, jnp.arange(slot_table.shape[0], dtype=jnp.int32)[None, :], 0), axis=1)
    return tile, live


ROUND = 8


def all_tiles(gathered):
    heads, _, width = gathered.shape
    tiles = gathered.reshape(heads, 3, HEAD, width // 64, 2, 32).transpose(3, 1, 0, 5, 4, 2)
    return tiles.reshape(-1, 32, 128)


def pack_kernel(place_ref, grad, out):
    lane = lax.broadcasted_iota(jnp.int32, (32, 128), 1) < 64
    rows, width = grad.shape
    for part in range(rows // 64):
        for pair in range(width // 128):
            both = grad[part * 64 : part * 64 + 64, pair * 128 : pair * 128 + 128].astype(F32).T
            for odd in range(2):
                tile = both[odd * 64 : odd * 64 + 64]
                wide = jnp.concatenate([tile[0:32], tile[32:64]], axis=1)
                out[place_ref[part * (width // 64) + pair * 2 + odd]] = wide.astype(BF)


def pack_tiles(place, grad, count):
    return pl.pallas_call(
        pack_kernel,
        out_shape=jax.ShapeDtypeStruct((count + 1, 32, 128), BF),
        in_specs=[SM, VM],
        out_specs=VM,
        compiler_params=pltpu.CompilerParams(vmem_limit_bytes=16 << 20),
        cost_estimate=pl.CostEstimate(flops=1 << 30, bytes_accessed=2 << 20, transcendentals=0),
        name="pack_tiles",
    )(place, grad)


def send_tiles(slot_table, slot_cap, grad, own):
    ctx_size, fsdp_size = lax.axis_size("ctx"), lax.axis_size("fsdp")
    ctx_index, fsdp_index = lax.axis_index("ctx"), lax.axis_index("fsdp")
    across = grad.shape[1] // 64
    heads, per = ctx_size, 3 * across
    owner = (slot_table[: 3 * across * heads] // slot_cap).reshape(across, 3, heads).transpose(2, 1, 0).reshape(heads, per)
    earlier = jnp.arange(per)[:, None] > jnp.arange(per)[None, :]
    rank = jnp.sum(((owner[:, :, None] == owner[:, None, :]) & earlier[None]).astype(jnp.int32), axis=2)
    mine, my_rank = owner[ctx_index], rank[ctx_index]
    to_us = mine % fsdp_size == fsdp_index

    here = to_us & (my_rank < ROUND)
    place = jnp.where(here, (mine // fsdp_size) * ROUND + my_rank, ctx_size * ROUND)
    packed = pack_tiles(place, grad, ctx_size * ROUND)[: ctx_size * ROUND]
    got = lax.all_to_all(packed.reshape(ctx_size, ROUND, 32, 128), "ctx", 0, 0, tiled=True)

    def whole(grad):
        return all_tiles(lax.all_gather(grad[None], "ctx", axis=0, tiled=True))

    rest = lax.cond(
        jnp.max(rank) >= ROUND, whole, lambda grad: jnp.zeros((heads * per, 32, 128), BF), after(grad, got)
    )
    row, part, head = own // (3 * heads), (own // heads) % 3, own % heads
    own_rank = rank.reshape(-1)[jnp.clip(head * per + part * across + row, 0, heads * per - 1)]
    early = own_rank < ROUND
    place = jnp.where(early, head * ROUND + own_rank, ctx_size * ROUND + own)
    return jnp.concatenate([got.reshape(-1, 32, 128), rest], axis=0), place, got


def gain_step(grads_in, gains_old, first_old, second_old):
    first_new = beta_one * first_old + (1.0 - beta_one) * grads_in
    second_new = beta_two * second_old + (1.0 - beta_two) * grads_in * grads_in
    gains_new = gains_old - gain_rate * first_new / (jnp.sqrt(second_new) + adam_eps)
    return (gains_new, first_new, second_new)


def on_device(
    inputs,
    cotangent,
    segments,
    w_qkv,
    w_out,
    w_in,
    w_down,
    norm_gains,
    slot_table,
    master,
    first_moment,
    rotated_second_moments,
    row_eigenbasis,
    column_eigenbasis,
    gain_master,
    gain_first,
    gain_second,
):
    micro, shard, width = inputs.shape
    heads = width // HEAD
    full_len = segments.shape[1]
    ctx_size = lax.axis_size("ctx")
    ctx_index = lax.axis_index("ctx")
    copies = max(1, ctx_size // heads)

    def spread(x):
        if copies > 1:
            x = jnp.repeat(x, copies, axis=0)
        return lax.all_to_all(x, "ctx", 0, 0, tiled=True)

    def collect(x):
        x = lax.all_to_all(x, "ctx", 0, 0, tiled=True)
        return x[::copies] if copies > 1 else x

    gains = lax.all_gather(norm_gains, "fsdp", axis=1, tiled=True).astype(F32)
    fast_gather = two_parts()
    if fast_gather:
        got_qkv = swap_bit(own_piece(w_qkv), "fsdp", 1)
        full_qkv = joined(w_qkv, got_qkv, swap_bit(got_qkv, "ctx", 1))
        later = [w_out, w_in, w_down]
        got_later = [swap_bit(after(own_piece(w), got_qkv), "fsdp", 1) for w in later]
    else:
        full_qkv, full_out, full_in, full_down = (
            lax.all_gather(w, "fsdp", axis=0, tiled=True) for w in (w_qkv, w_out, w_in, w_down)
        )

    qkv_all, tables, normed_all, layer_ins, sends = [], [], [], [], []
    for b in range(micro):
        seg_all = segments[b]
        positions = doc_positions(seg_all)
        tables.append(positions)
        own_cos, own_sin = rope_tables(lax.dynamic_slice_in_dim(positions, ctx_index * shard, shard))
        layer_in = inputs[b].astype(F32)
        normed = layer_norm(layer_in, gains[0]).astype(BF)
        proj = mm(full_qkv, normed, 0, 1).reshape(3, heads, HEAD, shard)

        def rotate(v, scale):
            a, c = v[:, : HEAD // 2], v[:, HEAD // 2 :]
            return jnp.concatenate([a * own_cos - c * own_sin, c * own_cos + a * own_sin], axis=1) * scale

        send = jnp.concatenate(
            [rotate(proj[0], LOG2E * HEAD**-0.5).astype(BF), rotate(proj[1], 1.0).astype(BF), proj[2].astype(BF)],
            axis=1,
        )
        sends.append(send)
        qkv_all.append(spread(send))
        normed_all.append(normed)
        layer_ins.append(layer_in)

    tables = [rope_tables(after(p, *sends)) for p in tables]
    attended_all, raw_all, outs = [], [], []
    for b in range(micro):
        ready = after(qkv_all[b], *(outs[-1:] or sends))
        out, raw, lse = attend_forward(ready, segments[b], bq=min(1024, full_len), bk=512, sub=min(1024, full_len))
        outs.append(out)
        raw_all.append((raw, lse))
        attended_all.append(collect(out).reshape(width, shard))
    wide = lax.all_gather(after(jnp.stack(normed_all), qkv_all[-1]), "ctx", axis=1, tiled=True)
    normed_wide = [wide[b] for b in range(micro)]
    if fast_gather:
        got_later = [after(g, outs[0]) for g in got_later]
        twins = [after(swap_bit(g, "ctx", 1), outs[-1]) for g in got_later]
        full_out, full_in, full_down = (joined(*parts) for parts in zip(later, got_later, twins))

    results, d_middles, d_att_all = [], [], []
    hidden_all, d_gate_all, normed_two_all, branch_all = [], [], [], []
    gain_two_sum = 0.0
    for b in range(micro):
        if b:
            attended_all[b] = after(attended_all[b], branch_all[b - 1])
        middle_value = layer_ins[b] + mm(attended_all[b], full_out, 0, 0)
        normed_two = layer_norm(middle_value, gains[1]).astype(BF)
        gate_up = mm(normed_two, full_in, 1, 0)
        grad_top = cotangent[b]
        d_hidden = mm(grad_top, full_down, 1, 1)
        hidden, d_gate_up = gated_both(gate_up, d_hidden)
        hidden, d_gate_up = hidden.astype(BF), d_gate_up.astype(BF)
        results.append((middle_value, hidden))
        d_normed_two = mm(d_gate_up, full_in, 1, 1)
        d_mid_norm, gain_two = norm_back(middle_value, gains[1], d_normed_two)
        d_middle = grad_top.astype(F32) + d_mid_norm
        grad_branch = d_middle.astype(BF)
        d_att = mm(full_out, grad_branch, 1, 1).astype(BF).reshape(heads, HEAD, shard)
        d_att_all.append(spread(d_att))
        d_middles.append(d_middle)
        hidden_all.append(hidden)
        d_gate_all.append(d_gate_up)
        normed_two_all.append(normed_two)
        branch_all.append(grad_branch)
        gain_two_sum = gain_two_sum + gain_two

    def rows(parts):
        return jnp.concatenate(parts, axis=0)

    grad_out = mm(jnp.concatenate(attended_all, axis=1), rows(branch_all), 1, 0).astype(BF)
    grad_in = mm(rows(normed_two_all), rows(d_gate_all), 0, 0).astype(BF)
    grad_down = mm(rows(hidden_all), cotangent.reshape(-1, width), 0, 0).astype(BF)
    slot_cap = master.shape[0]
    slot_total = slot_cap * ctx_size * lax.axis_size("fsdp")
    where = after(slot_table[3 * (width // 64) ** 2 :], d_att_all[0])
    fast = halving_applies() and micro == 2
    waits = [()] * micro
    if fast:
        owner = where // slot_cap
        rest = where % slot_cap
        cut = slot_cap // 2
        low = rest < cut
        core = (owner // 2) % 2
        x_rel = (owner % 2) ^ lax.axis_index("fsdp")
        ctx_rel = (owner // 2) ^ ctx_index
        y_rel, z_one, z_two = (ctx_rel // 2) % 2, (ctx_rel // 4) % 2, ctx_rel // 8
        z_rel = z_one * 2 + z_two
        place = jnp.where(
            low,
            ((x_rel * 2 + y_rel) * 4 + z_rel) * cut + rest,
            16 * cut + ((y_rel * 2 + x_rel) * 4 + z_rel) * (slot_cap - cut) + rest - cut,
        )
        where = place + jnp.where(core == ctx_index % 2, slot_total // 2, 0)
        send, keep = scatter_tiles([grad_out, grad_in, grad_down], where, slot_total, 2)
        got = swap_bit(send, "ctx", 1)

        def both(low, high):
            return keep[low:high] + got[low:high]

        ours = [both(0, 8 * cut), both(16 * cut, 16 * cut + 8 * (slot_cap - cut))]
        theirs = [both(8 * cut, 16 * cut), both(16 * cut + 8 * (slot_cap - cut), 16 * slot_cap)]
        near = [swap_bit(theirs[0], "fsdp", 1), swap_bit(theirs[1], "ctx", 2)]
        waits[0] = (*ours, *theirs)
    else:
        (slotted,) = scatter_tiles([grad_out, grad_in, grad_down], where, slot_total, 1)
        own_slots = lax.psum_scatter(slotted, ("ctx", "fsdp"), scatter_dimension=0, tiled=True)

    d_proj_all, grad_heads = [], 0.0
    for b in range(micro):
        cosine, sine = tables[b]
        d_att = after(d_att_all[b], *waits[b])
        grads, flat = attend_backward(
            qkv_all[b], segments[b], d_att, *raw_all[b], cosine, sine, bq=512, bk=512, sub=512
        )
        if fast and b == 0:
            near = [after(v, grads) for v in near]
            next_ours = [t[: t.shape[0] // 2] + v[: t.shape[0] // 2] for t, v in zip(ours, near)]
            next_theirs = [t[t.shape[0] // 2 :] + v[t.shape[0] // 2 :] for t, v in zip(ours, near)]
            next_near = [swap_bit(next_theirs[0], "ctx", 2), swap_bit(next_theirs[1], "fsdp", 1)]
            waits[1] = (*next_ours, *next_theirs)
        elif fast:
            next_near = [after(v, grads) for v in next_near]
            pair = [(t.reshape(2, 2, -1, 32, 128), v.reshape(2, 2, -1, 32, 128)) for t, v in zip(next_ours, next_near)]
            kept, sent = (jnp.concatenate([t[side] + v[side] for t, v in pair], axis=1) for side in (0, 1))
            flat = after(flat, sent)
            got = swap_bit(sent, "ctx", 4)
            kept, sent = (kept[side] + got[side] for side in (0, 1))
            first_turn = got
            own_slots = kept + swap_bit(sent, "ctx", 8)
        last_grads = grads
        if b + 1 < micro:
            d_proj_all.append(collect(grads))
        grad_heads = grad_heads + mm(flat, normed_wide[b], 1, 0)

    states = [master, first_moment, rotated_second_moments, row_eigenbasis, column_eigenbasis]
    outputs_list = [(m + mm(h, full_down, 1, 0)).astype(BF) for m, h in results]
    own, live = own_tiles(slot_table, slot_cap)
    is_qkv = own < 3 * heads * (width // 64)
    share = lax.dynamic_index_in_dim(full_qkv.reshape(width, 3, heads, HEAD), ctx_index // copies, 2, keepdims=False)
    gain_one = jnp.sum(grad_heads * share.reshape(width, 3 * HEAD).T.astype(F32), axis=0) / (gains[0] * copies)
    grad_heads = after(grad_heads.astype(BF), d_proj_all[0], *(next_near if fast else ()))
    if fast and heads == ctx_size:
        grad_heads = after(grad_heads + swap_bit(grad_heads, "fsdp", 1), first_turn)
        pool, place, first_round = send_tiles(slot_table, slot_cap, grad_heads, own)
        last_grads = after(last_grads, first_round, own_slots, pool, *outputs_list)
    else:
        grad_heads = lax.psum(grad_heads, "fsdp")
        pool = all_tiles(lax.all_gather(grad_heads[None], "ctx", axis=0, tiled=True)[::copies])
        place = own
    d_proj_all.append(collect(last_grads))
    picks = (is_qkv.astype(jnp.int32), jnp.where(is_qkv, place, 0), live)

    input_grads = []
    for b in range(micro):
        d_proj = d_proj_all[b].reshape(heads, 3, HEAD, shard).transpose(1, 0, 2, 3).reshape(3 * width, shard)
        d_normed = mm(d_proj, full_qkv, 0, 1)
        d_in_norm, _ = norm_back(layer_ins[b], gains[0], d_normed)
        input_grads.append((d_middles[b] + d_in_norm).astype(BF))
    gain_grads = sum_all(after(jnp.stack([gain_one, gain_two_sum]), d_proj_all[-1]))

    own_grads, new_master, new_copy, new_first, new_second = soap_step(
        picks, pool, own_slots, *states
    )
    new_gains, new_gain_first, new_gain_second = gain_step(gain_grads, gain_master, gain_first, gain_second)
    return (
        jnp.stack(outputs_list),
        jnp.stack(input_grads),
        own_grads,
        gain_grads,
        new_master,
        new_copy,
        new_first,
        new_second,
        new_gains,
        new_gain_first,
        new_gain_second,
    )


def solution(mesh):
    tokens = P("fsdp", "ctx", None)
    slots = P(("ctx", "fsdp"), None, None)
    placed = (
        tokens,
        tokens,
        *(P("fsdp", None),) * 5,
        P(None, "fsdp"),
        P(),
        *(slots,) * 5,
        *(P(),) * 3,
    )
    return jax.shard_map(
        on_device,
        mesh=mesh,
        in_specs=placed,
        out_specs=(tokens, tokens, slots, P(), slots, slots, slots, slots, P(), P(), P()),
        check_vma=False,
    )
```

```python
import functools
import jax, jax.numpy as jnp
from jax import lax
from jax.experimental import pallas as pl
from jax.experimental.pallas import tpu as pltpu
from jax.sharding import PartitionSpec as P

HEAD = 64
NDOC=8
BIG=1e30
LN2=0.6931471805599453
LOG2E=1.4426950408889634

def split3(v):
    hi=v.astype(jnp.bfloat16)
    r=v-hi.astype(jnp.float32)
    mid=r.astype(jnp.bfloat16)
    lo=(r-mid.astype(jnp.float32)).astype(jnp.bfloat16)
    return hi.astype(jnp.float32),mid.astype(jnp.float32),lo.astype(jnp.float32)

def doc_rows(seg_row):
    n=seg_row.shape[1]
    ids=lax.broadcasted_iota(jnp.int32,(NDOC,n),0)
    return (ids==seg_row).astype(jnp.float32)

def fwd_kernel(bq,bk,sub,lo_ref,hi_ref,qkv_ref,seg_ref,out_ref,raw_ref,lse_ref,q_s,k_s,v_s):
    chunks,_,width=qkv_ref.shape
    full=chunks*width
    def prep(c,carry):
        cols=pl.ds(pl.multiple_of(c*width,width),width)
        hot=doc_rows(seg_ref[:,cols])
        zero8=jnp.zeros((8,width),jnp.float32)
        q_s[0:64,cols]=qkv_ref[c,0:64,:]
        q_s[64:80,cols]=jnp.concatenate([hot,zero8],0).astype(jnp.bfloat16)
        kt=jnp.concatenate([qkv_ref[c,64:128,:].astype(jnp.float32),(hot-1.0)*BIG,jnp.zeros((56,width),jnp.float32)],0)
        k_s[cols,:]=kt.T.astype(jnp.bfloat16)
        v_s[0:64,cols]=qkv_ref[c,128:192,:]
        row=lax.broadcasted_iota(jnp.int32,(16,width),0)
        v_s[64:80,cols]=(row==0).astype(jnp.bfloat16)
        return carry
    lax.fori_loop(0,chunks,prep,0)
    def q_step(i,carry):
        cols=pl.ds(pl.multiple_of(i*bq,bq),bq)
        qa=q_s[:,cols]
        def k_step(j,state):
            rows=pl.ds(pl.multiple_of(j*bk,bk),bk)
            ka=k_s[rows,0:80]
            va=v_s[:,rows]
            new=[]
            for n in range(bq//sub):
                m,acc=state[n]
                s=jnp.dot(ka,qa[:,n*sub:(n+1)*sub],preferred_element_type=jnp.float32)
                m_new=jnp.maximum(m,jnp.max(s,axis=0,keepdims=True))
                p=jnp.exp2(s-m_new).astype(jnp.bfloat16)
                acc=acc*jnp.exp2(m-m_new)+jnp.dot(va,p,preferred_element_type=jnp.float32)
                new.append((m_new,acc))
            return tuple(new)
        init=tuple((jnp.full((1,sub),-3e38,jnp.float32),jnp.zeros((80,sub),jnp.float32)) for _ in range(bq//sub))
        state=lax.fori_loop(lo_ref[i],hi_ref[i],k_step,init)
        m=jnp.concatenate([s[0] for s in state],1); acc=jnp.concatenate([s[1] for s in state],1)
        total=acc[64:65]
        o=acc[0:64]/total
        raw_ref[:,cols]=o
        lse_ref[:,cols]=m+jnp.log2(total)
        return carry
    lax.fori_loop(0,full//bq,q_step,0)
    def emit(c,carry):
        cols=pl.ds(pl.multiple_of(c*width,width),width)
        out_ref[c]=raw_ref[:,cols].astype(jnp.bfloat16)
        return carry
    lax.fori_loop(0,chunks,emit,0)

def bwd_kernel(bq,bk,sub,lo_ref,hi_ref,qkv_ref,seg_ref,do_ref,raw_ref,lse_ref,cos_ref,sin_ref,out_ref,flat_ref,
               q_s,kt_s,k_s,vt_s,do_s,qdt_s,dkv_s):
    chunks,_,width=qkv_ref.shape
    full=chunks*width
    def prep(c,carry):
        cols=pl.ds(pl.multiple_of(c*width,width),width)
        hot=doc_rows(seg_ref[:,cols])
        row=lax.broadcasted_iota(jnp.int32,(8,width),0)
        ones3=(row<3).astype(jnp.float32)
        def three(v):
            a,b,d=split3(-v)
            return jnp.where(row==0,a,jnp.where(row==1,b,jnp.where(row==2,d,0.0)))
        qt=qkv_ref[c,0:64,:]
        kt=qkv_ref[c,64:128,:]
        dt=do_ref[c]
        kt_s[0:64,cols]=kt
        kt_s[64:80,cols]=jnp.concatenate([(hot-1.0)*BIG,ones3],0).astype(jnp.bfloat16)
        vt_s[0:64,cols]=qkv_ref[c,128:192,:]
        vt_s[64:80,cols]=jnp.concatenate([ones3,jnp.zeros((8,width),jnp.float32)],0).astype(jnp.bfloat16)
        qdt_s[0:64,cols]=qt
        qdt_s[64:128,cols]=dt
        qq=jnp.concatenate([qt.astype(jnp.float32),hot,three(lse_ref[:,cols]),jnp.zeros((48,width),jnp.float32)],0)
        q_s[cols,:]=qq.T.astype(jnp.bfloat16)
        df=dt.astype(jnp.float32)
        delta=jnp.sum(df*raw_ref[:,cols],axis=0,keepdims=True)
        dd=jnp.concatenate([df,three(delta),jnp.zeros((56,width),jnp.float32)],0)
        do_s[cols,:]=dd.T.astype(jnp.bfloat16)
        kk=jnp.concatenate([kt.astype(jnp.float32),jnp.zeros((64,width),jnp.float32)],0)
        k_s[cols,:]=kk.T.astype(jnp.bfloat16)
        dkv_s[:,cols]=jnp.zeros((128,width),jnp.float32)
        return carry
    lax.fori_loop(0,chunks,prep,0)
    def q_step(i,carry):
        cols=pl.ds(pl.multiple_of(i*bq,bq),bq)
        qt=qdt_s[0:64,cols]; dt=qdt_s[64:128,cols]
        def k_step(j,dq):
            keys=pl.ds(pl.multiple_of(j*bk,bk),bk)
            dqs=[]; ps=[]; dss=[]
            for r in range(bq//sub):
                rr=pl.ds(pl.multiple_of(i*bq+r*sub,sub),sub)
                s=jnp.dot(q_s[rr,0:80],kt_s[:,keys],preferred_element_type=jnp.float32)
                dp=jnp.dot(do_s[rr,0:80],vt_s[:,keys],preferred_element_type=jnp.float32)
                p=jnp.exp2(s)
                ps.append(p.astype(jnp.bfloat16))
                ds=(p*dp).astype(jnp.bfloat16)
                dss.append(ds)
                dqs.append(jnp.dot(ds,k_s[keys,:],preferred_element_type=jnp.float32))
            ds=jnp.concatenate(dss,0); p16=jnp.concatenate(ps,0)
            dkv_s[0:64,keys]+=jnp.dot(qt,ds,preferred_element_type=jnp.float32)
            dkv_s[64:128,keys]+=jnp.dot(dt,p16,preferred_element_type=jnp.float32)
            return dq+jnp.concatenate(dqs,0)
        dq=lax.fori_loop(lo_ref[i],hi_ref[i],k_step,jnp.zeros((bq,128),jnp.float32))
        dq=(dq*0.125).T[0:64]
        c=cos_ref[:,cols]; s=sin_ref[:,cols]
        a,b=dq[0:32],dq[32:64]
        rot=jnp.concatenate([a*c+b*s,b*c-a*s],0).astype(jnp.bfloat16)
        flat_ref[0:64,cols]=rot
        return carry
    lax.fori_loop(0,full//bq,q_step,0)
    def emit(c,carry):
        cols=pl.ds(pl.multiple_of(c*width,width),width)
        t=dkv_s[:,cols]
        dk=t[0:64]*LN2
        co=cos_ref[:,cols]; si=sin_ref[:,cols]
        a,b=dk[0:32],dk[32:64]
        v=jnp.concatenate([a*co+b*si,b*co-a*si,t[64:128]],0).astype(jnp.bfloat16)
        flat_ref[64:192,cols]=v
        out_ref[c,0:64,:]=flat_ref[0:64,cols]
        out_ref[c,64:192,:]=v
        return carry
    lax.fori_loop(0,chunks,emit,0)

def ranges(seg_row,bq,bk):
    full=seg_row.shape[0]
    firsts=seg_row[::bq]; lasts=seg_row[bq-1::bq]
    lo=jnp.sum((seg_row[None,:]<firsts[:,None]).astype(jnp.int32),axis=1)//bk
    hi=-(-jnp.sum((seg_row[None,:]<=lasts[:,None]).astype(jnp.int32),axis=1)//bk)
    return lo.astype(jnp.int32),hi.astype(jnp.int32)

VM=pl.BlockSpec(memory_space=pltpu.VMEM)
SM=pl.BlockSpec(memory_space=pltpu.SMEM)
def attend_forward(qkv,seg_row,bq=512,bk=512,sub=256):
    chunks,_,width=qkv.shape; full=chunks*width
    lo,hi=ranges(seg_row,bq,bk)
    return pl.pallas_call(functools.partial(fwd_kernel,bq,bk,sub),
      out_shape=(jax.ShapeDtypeStruct((chunks,64,width),jnp.bfloat16),jax.ShapeDtypeStruct((64,full),jnp.float32),jax.ShapeDtypeStruct((1,full),jnp.float32)),
      in_specs=[SM,SM,VM,VM],out_specs=(VM,VM,VM),
      scratch_shapes=[pltpu.VMEM((80,full),jnp.bfloat16),pltpu.VMEM((full,128),jnp.bfloat16),pltpu.VMEM((80,full),jnp.bfloat16)],
      compiler_params=pltpu.CompilerParams(vmem_limit_bytes=40<<20),
      cost_estimate=pl.CostEstimate(flops=1140*full*full,bytes_accessed=8<<20,transcendentals=0),
      name="attend_fwd")(lo,hi,qkv,seg_row[None,:])
def attend_backward(qkv,seg_row,do,raw,lse,cos,sin,bq=512,bk=512,sub=512):
    chunks,_,width=qkv.shape; full=chunks*width
    lo,hi=ranges(seg_row,bq,bk)
    return pl.pallas_call(functools.partial(bwd_kernel,bq,bk,sub),
      out_shape=(jax.ShapeDtypeStruct((chunks,192,width),jnp.bfloat16),jax.ShapeDtypeStruct((192,full),jnp.bfloat16)),
      in_specs=[SM,SM,VM,VM,VM,VM,VM,VM,VM],out_specs=(VM,VM),
      scratch_shapes=[pltpu.VMEM((full,128),jnp.bfloat16),pltpu.VMEM((80,full),jnp.bfloat16),pltpu.VMEM((full,128),jnp.bfloat16),
        pltpu.VMEM((80,full),jnp.bfloat16),pltpu.VMEM((full,128),jnp.bfloat16),pltpu.VMEM((128,full),jnp.bfloat16),pltpu.VMEM((128,full),jnp.float32)],
      compiler_params=pltpu.CompilerParams(vmem_limit_bytes=56<<20),
      cost_estimate=pl.CostEstimate(flops=1580*full*full,bytes_accessed=16<<20,transcendentals=0),
      name="attend_bwd")(lo,hi,qkv,seg_row[None,:],do,raw,lse,cos,sin)

FF = 2624
BLOCK_ORDER = 64
rope_base = 160000.0
norm_eps = 1e-05
adam_eps = 1e-08
beta_one = 0.5
beta_two = 0.5
block_rate = 0.03
gain_rate = 0.75
decay_rate = 0.01
BF = jnp.bfloat16
F32 = jnp.float32


def layer_norm(values, gain_row):
    center = values - jnp.mean(values, axis=-1, keepdims=True)
    spread = jnp.mean(center * center, axis=-1, keepdims=True)
    return center * lax.rsqrt(spread + norm_eps) * gain_row


def norm_back(values, gain_row, grad_rows):
    unused, pullback = jax.vjp(layer_norm, values, gain_row)
    return pullback(grad_rows)


def doc_positions(seg_row):
    doc_ids = jnp.arange(NDOC, dtype=jnp.int32)
    matches = seg_row[:, None] == doc_ids[None, :]
    counts = jnp.sum(matches.astype(jnp.int32), axis=0)
    starts = jnp.cumsum(counts) - counts
    doc_begin = jnp.sum(jnp.where(matches, starts[None, :], 0), axis=1)
    return jnp.arange(seg_row.shape[0], dtype=jnp.int32) - doc_begin


def rope_tables(positions):
    half = HEAD // 2
    frequency = rope_base ** (-(jnp.arange(half, dtype=F32) * 2.0) / HEAD)
    angles = positions.astype(F32)[None, :] * frequency[:, None]
    return jnp.cos(angles), jnp.sin(angles)


def gated_gelu(gate_up):
    return jax.nn.gelu(gate_up[:, :FF], approximate=False) * gate_up[:, FF:]


def gated_both(gate_up, grad_hidden):
    hidden, pullback = jax.vjp(gated_gelu, gate_up)
    return hidden, pullback(grad_hidden)[0]


def mm(a, b, da, db):
    return lax.dot_general(a, b, (((da,), (db,)), ((), ())), preferred_element_type=F32)


def after(x, *others):
    return lax.optimization_barrier((x, *others))[0]


def swap_bit(x, axis, bit):
    n = lax.axis_size(axis)
    return lax.ppermute(x, axis, [(s, s ^ bit) for s in range(n)])


def two_parts():
    return lax.axis_size("fsdp") == 2 and lax.axis_size("ctx") % 2 == 0


def own_piece(shard):
    half = shard.shape[0] // 2
    return lax.dynamic_slice_in_dim(shard, (lax.axis_index("ctx") % 2) * half, half)


def joined(shard, got, twin):
    first = lax.axis_index("ctx") % 2 == 0
    mine = lax.axis_index("fsdp") == 0
    other = jnp.concatenate([jnp.where(first, got, twin), jnp.where(first, twin, got)], axis=0)
    return jnp.concatenate([jnp.where(mine, shard, other), jnp.where(mine, other, shard)], axis=0)


def halving_applies():
    return lax.axis_size("ctx") == 16 and lax.axis_size("fsdp") == 2


def half_of(x, axis, bit):
    return lax.dynamic_index_in_dim(x, bit, axis, keepdims=False)


def sum_all(x):
    for name in ("ctx", "fsdp"):
        for b in range(lax.axis_size(name).bit_length() - 1):
            x = x + swap_bit(x, name, 1 << b)
    return x


def scatter_kernel(counts, parts, where_ref, *refs):
    n = len(counts)
    grads, outs, stage, sems = refs[:n], refs[n : n + parts], refs[n + parts], refs[n + parts + 1]
    lane = lax.broadcasted_iota(jnp.int32, (32, 128), 1) < 64
    size = outs[0].shape[0]
    base = 0
    for grad, (row_tiles, col_tiles) in zip(grads, counts):

        def drain(buf):
            pltpu.make_async_copy(
                stage.at[buf, pl.ds(0, col_tiles)], outs[0].at[pl.ds(0, col_tiles)], sems.at[buf]
            ).wait()

        def strip(i, carry, grad=grad, base=base, col_tiles=col_tiles, drain=drain):
            buf = lax.rem(i, 2)

            @pl.when(i >= 2)
            def _():
                drain(buf)

            top = pl.ds(pl.multiple_of(i * 64, 64), 32)
            bottom = pl.ds(pl.multiple_of(i * 64 + 32, 32), 32)
            for j in range(col_tiles // 2):
                a = grad[top, j * 128 : (j + 1) * 128].astype(F32)
                b = grad[bottom, j * 128 : (j + 1) * 128].astype(F32)
                stage[buf, 2 * j] = jnp.where(lane, a, pltpu.roll(b, 64, 1)).astype(BF)
                stage[buf, 2 * j + 1] = jnp.where(lane, pltpu.roll(a, 64, 1), b).astype(BF)
            for j in range(col_tiles):
                place = where_ref[base + i * col_tiles + j]
                if parts == 1:
                    pltpu.make_async_copy(stage.at[buf, j], outs[0].at[place], sems.at[buf]).start()
                else:

                    @pl.when(place < size)
                    def _(j=j, place=place):
                        pltpu.make_async_copy(stage.at[buf, j], outs[0].at[place], sems.at[buf]).start()

                    @pl.when(place >= size)
                    def _(j=j, place=place):
                        pltpu.make_async_copy(stage.at[buf, j], outs[1].at[place - size], sems.at[buf]).start()

            return carry

        lax.fori_loop(0, row_tiles, strip, 0)
        drain((row_tiles - 2) % 2)
        drain((row_tiles - 1) % 2)
        base += row_tiles * col_tiles


def scatter_tiles(grads, where, total, parts):
    counts = tuple((g.shape[0] // 64, g.shape[1] // 64) for g in grads)
    widest = max(c for _, c in counts)
    return pl.pallas_call(
        functools.partial(scatter_kernel, counts, parts),
        out_shape=(jax.ShapeDtypeStruct((total // parts, 32, 128), BF),) * parts,
        in_specs=[SM] + [VM] * len(grads),
        out_specs=(pl.BlockSpec(memory_space=pl.ANY),) * parts,
        scratch_shapes=[pltpu.VMEM((2, widest, 32, 128), BF), pltpu.SemaphoreType.DMA((2,))],
        compiler_params=pltpu.CompilerParams(vmem_limit_bytes=48 << 20),
        cost_estimate=pl.CostEstimate(flops=40 << 30, bytes_accessed=40 << 20, transcendentals=0),
        name="scatter_tiles",
    )(where, *grads)


def soap_kernel(block, kind_ref, pick_ref, live_ref, pool, rest, early, master, first, second, left, right,
                grads_out, master_out, copy_out, first_out, second_out, tiles, sem):
    step = pl.program_id(0)
    total = tiles.shape[0]

    @pl.when(step == 0)
    def _():
        def fetch(n, carry):
            pick = pick_ref[n]

            @pl.when(pick < pool.shape[0])
            def _():
                pltpu.make_async_copy(pool.at[pick], tiles.at[n], sem).start()

            @pl.when(pick >= pool.shape[0])
            def _():
                pltpu.make_async_copy(rest.at[pick - pool.shape[0]], tiles.at[n], sem).start()

            return carry

        lax.fori_loop(0, total, fetch, 0)
        pltpu.make_async_copy(tiles, tiles, sem).wait()

    def two(v):
        hi = v.astype(BF)
        return hi, (v - hi.astype(F32)).astype(BF)

    def product(a, b):
        ah, al = two(a)
        bh, bl = two(b)
        return jnp.dot(
            jnp.concatenate([ah, ah, al], axis=1), jnp.concatenate([bh, bl, bh], axis=0), preferred_element_type=F32
        )

    def each(f, *lists):
        return [f(*row) for row in zip(*lists)]

    for low in range(0, block, 8):
        group = range(low, min(low + 8, block))

        def own_tile(k):
            n = jnp.minimum(step * block + k, total - 1)
            flat = jnp.where(kind_ref[n] != 0, tiles[n].astype(F32), early[k].astype(F32))
            tile = jnp.concatenate([flat[:, 0:64], flat[:, 64:128]], axis=0)
            return jnp.where(live_ref[n] != 0, tile, 0.0)

        lives = [live_ref[jnp.minimum(step * block + k, total - 1)] != 0 for k in group]
        tile_list = [own_tile(k) for k in group]
        half = each(lambda k, t: product(left[k].T, t), group, tile_list)
        turned = each(lambda k, t: product(t, right[k]), group, half)
        firsts = each(lambda k, t: beta_one * first[k] + (1.0 - beta_one) * t, group, turned)
        seconds = each(lambda k, t: beta_two * second[k] + (1.0 - beta_two) * t * t, group, turned)
        normal = each(lambda f, s: f / (jnp.sqrt(s) + adam_eps), firsts, seconds)
        half = each(lambda k, t: product(left[k], t), group, normal)
        restored = each(lambda k, t: product(t, right[k].T), group, half)
        for k, live, tile, f, s, r in zip(group, lives, tile_list, firsts, seconds, restored):
            weights = master[k]
            new = jnp.where(live, weights - block_rate * (r + decay_rate * weights), weights)
            grads_out[k] = tile
            master_out[k] = new
            copy_out[k] = new.astype(BF)
            first_out[k] = jnp.where(live, f, first[k])
            second_out[k] = jnp.where(live, s, second[k])


def soap_step(picks, pools, early, master, first, second, left, right):
    cap = master.shape[0]
    block = min(16, cap)
    spec = pl.BlockSpec((block, 64, 64), lambda i: (i, 0, 0))
    whole = pl.BlockSpec(memory_space=pl.ANY)
    like = jax.ShapeDtypeStruct(master.shape, F32)
    return pl.pallas_call(
        functools.partial(soap_kernel, block),
        grid=(-(-cap // block),),
        out_shape=(like, like, jax.ShapeDtypeStruct(master.shape, BF), like, like),
        in_specs=[SM] * 3 + [whole] * 2 + [pl.BlockSpec((block, 32, 128), lambda i: (i, 0, 0))] + [spec] * 5,
        out_specs=(spec,) * 5,
        scratch_shapes=[pltpu.VMEM((cap, 32, 128), BF), pltpu.SemaphoreType.DMA],
        compiler_params=pltpu.CompilerParams(vmem_limit_bytes=40 << 20),
        cost_estimate=pl.CostEstimate(flops=23 << 30, bytes_accessed=30 << 20, transcendentals=0),
        name="soap",
    )(*picks, *pools, early, master, first, second, left, right)


def own_tiles(slot_table, slot_cap):
    device_index = lax.axis_index(("ctx", "fsdp"))
    own_ids = device_index * slot_cap + jnp.arange(slot_cap, dtype=jnp.int32)
    hit = slot_table[None, :] == own_ids[:, None]
    live = jnp.any(hit, axis=1).astype(jnp.int32)
    tile = jnp.sum(jnp.where(hit, jnp.arange(slot_table.shape[0], dtype=jnp.int32)[None, :], 0), axis=1)
    return tile, live


ROUND = 8


def all_tiles(gathered):
    heads, _, width = gathered.shape
    tiles = gathered.reshape(heads, 3, HEAD, width // 64, 2, 32).transpose(3, 1, 0, 5, 4, 2)
    return tiles.reshape(-1, 32, 128)


def pack_kernel(place_ref, grad, out):
    lane = lax.broadcasted_iota(jnp.int32, (32, 128), 1) < 64
    rows, width = grad.shape
    for part in range(rows // 64):
        for pair in range(width // 128):
            both = grad[part * 64 : part * 64 + 64, pair * 128 : pair * 128 + 128].astype(F32).T
            for odd in range(2):
                tile = both[odd * 64 : odd * 64 + 64]
                wide = jnp.concatenate([tile[0:32], tile[32:64]], axis=1)
                out[place_ref[part * (width // 64) + pair * 2 + odd]] = wide.astype(BF)


def pack_tiles(place, grad, count):
    return pl.pallas_call(
        pack_kernel,
        out_shape=jax.ShapeDtypeStruct((count + 1, 32, 128), BF),
        in_specs=[SM, VM],
        out_specs=VM,
        compiler_params=pltpu.CompilerParams(vmem_limit_bytes=16 << 20),
        cost_estimate=pl.CostEstimate(flops=1 << 30, bytes_accessed=2 << 20, transcendentals=0),
        name="pack_tiles",
    )(place, grad)


def send_tiles(slot_table, slot_cap, grad, own):
    ctx_size, fsdp_size = lax.axis_size("ctx"), lax.axis_size("fsdp")
    ctx_index, fsdp_index = lax.axis_index("ctx"), lax.axis_index("fsdp")
    across = grad.shape[1] // 64
    heads, per = ctx_size, 3 * across
    owner = (slot_table[: 3 * across * heads] // slot_cap).reshape(across, 3, heads).transpose(2, 1, 0).reshape(heads, per)
    earlier = jnp.arange(per)[:, None] > jnp.arange(per)[None, :]
    rank = jnp.sum(((owner[:, :, None] == owner[:, None, :]) & earlier[None]).astype(jnp.int32), axis=2)
    mine, my_rank = owner[ctx_index], rank[ctx_index]
    to_us = mine % fsdp_size == fsdp_index

    here = to_us & (my_rank < ROUND)
    place = jnp.where(here, (mine // fsdp_size) * ROUND + my_rank, ctx_size * ROUND)
    packed = pack_tiles(place, grad, ctx_size * ROUND)[: ctx_size * ROUND]
    got = lax.all_to_all(packed.reshape(ctx_size, ROUND, 32, 128), "ctx", 0, 0, tiled=True)

    def whole(grad):
        return all_tiles(lax.all_gather(grad[None], "ctx", axis=0, tiled=True))

    rest = lax.cond(
        jnp.max(rank) >= ROUND, whole, lambda grad: jnp.zeros((heads * per, 32, 128), BF), after(grad, got)
    )
    row, part, head = own // (3 * heads), (own // heads) % 3, own % heads
    own_rank = rank.reshape(-1)[jnp.clip(head * per + part * across + row, 0, heads * per - 1)]
    early = own_rank < ROUND
    place = jnp.where(early, head * ROUND + own_rank, ctx_size * ROUND + own)
    return (got.reshape(-1, 32, 128), rest), place, got


def gain_step(grads_in, gains_old, first_old, second_old):
    first_new = beta_one * first_old + (1.0 - beta_one) * grads_in
    second_new = beta_two * second_old + (1.0 - beta_two) * grads_in * grads_in
    gains_new = gains_old - gain_rate * first_new / (jnp.sqrt(second_new) + adam_eps)
    return (gains_new, first_new, second_new)


def on_device(
    inputs,
    cotangent,
    segments,
    w_qkv,
    w_out,
    w_in,
    w_down,
    norm_gains,
    slot_table,
    master,
    first_moment,
    rotated_second_moments,
    row_eigenbasis,
    column_eigenbasis,
    gain_master,
    gain_first,
    gain_second,
):
    micro, shard, width = inputs.shape
    heads = width // HEAD
    full_len = segments.shape[1]
    ctx_size = lax.axis_size("ctx")
    ctx_index = lax.axis_index("ctx")
    copies = max(1, ctx_size // heads)

    def spread(x):
        if copies > 1:
            x = jnp.repeat(x, copies, axis=0)
        return lax.all_to_all(x, "ctx", 0, 0, tiled=True)

    def collect(x):
        x = lax.all_to_all(x, "ctx", 0, 0, tiled=True)
        return x[::copies] if copies > 1 else x

    gains = lax.all_gather(norm_gains, "fsdp", axis=1, tiled=True).astype(F32)
    fast_gather = two_parts()
    if fast_gather:
        got_qkv = swap_bit(own_piece(w_qkv), "fsdp", 1)
        full_qkv = joined(w_qkv, got_qkv, swap_bit(got_qkv, "ctx", 1))
        later = [w_out, w_in, w_down]
        got_later = [swap_bit(after(own_piece(w), got_qkv), "fsdp", 1) for w in later]
    else:
        full_qkv, full_out, full_in, full_down = (
            lax.all_gather(w, "fsdp", axis=0, tiled=True) for w in (w_qkv, w_out, w_in, w_down)
        )

    qkv_all, tables, normed_all, layer_ins, sends = [], [], [], [], []
    for b in range(micro):
        seg_all = segments[b]
        positions = doc_positions(seg_all)
        tables.append(positions)
        own_cos, own_sin = rope_tables(lax.dynamic_slice_in_dim(positions, ctx_index * shard, shard))
        layer_in = inputs[b].astype(F32)
        normed = layer_norm(layer_in, gains[0]).astype(BF)
        proj = mm(full_qkv, normed, 0, 1).reshape(3, heads, HEAD, shard)

        def rotate(v, scale):
            a, c = v[:, : HEAD // 2], v[:, HEAD // 2 :]
            return jnp.concatenate([a * own_cos - c * own_sin, c * own_cos + a * own_sin], axis=1) * scale

        send = jnp.concatenate(
            [rotate(proj[0], LOG2E * HEAD**-0.5).astype(BF), rotate(proj[1], 1.0).astype(BF), proj[2].astype(BF)],
            axis=1,
        )
        sends.append(send)
        qkv_all.append(spread(send))
        normed_all.append(normed)
        layer_ins.append(layer_in)

    tables = [rope_tables(after(p, *sends)) for p in tables]
    attended_all, raw_all, outs = [], [], []
    for b in range(micro):
        ready = after(qkv_all[b], *(outs[-1:] or sends))
        out, raw, lse = attend_forward(ready, segments[b], bq=min(1024, full_len), bk=512, sub=min(1024, full_len))
        outs.append(out)
        raw_all.append((raw, lse))
        attended_all.append(collect(out).reshape(width, shard))
    wide = lax.all_gather(after(jnp.stack(normed_all), qkv_all[-1]), "ctx", axis=1, tiled=True)
    normed_wide = [wide[b] for b in range(micro)]
    if fast_gather:
        got_later = [after(g, outs[0]) for g in got_later]
        twins = [after(swap_bit(g, "ctx", 1), outs[-1]) for g in got_later]
        full_out, full_in, full_down = (joined(*parts) for parts in zip(later, got_later, twins))

    results, d_middles, d_att_all = [], [], []
    hidden_all, d_gate_all, normed_two_all, branch_all = [], [], [], []
    gain_two_sum = 0.0
    for b in range(micro):
        if b:
            attended_all[b] = after(attended_all[b], branch_all[b - 1])
        middle_value = layer_ins[b] + mm(attended_all[b], full_out, 0, 0)
        normed_two = layer_norm(middle_value, gains[1]).astype(BF)
        gate_up = mm(normed_two, full_in, 1, 0)
        grad_top = cotangent[b]
        d_hidden = mm(grad_top, full_down, 1, 1)
        hidden, d_gate_up = gated_both(gate_up, d_hidden)
        hidden, d_gate_up = hidden.astype(BF), d_gate_up.astype(BF)
        results.append((middle_value, hidden))
        d_normed_two = mm(d_gate_up, full_in, 1, 1)
        d_mid_norm, gain_two = norm_back(middle_value, gains[1], d_normed_two)
        d_middle = grad_top.astype(F32) + d_mid_norm
        grad_branch = d_middle.astype(BF)
        d_att = mm(full_out, grad_branch, 1, 1).astype(BF).reshape(heads, HEAD, shard)
        d_att_all.append(spread(d_att))
        d_middles.append(d_middle)
        hidden_all.append(hidden)
        d_gate_all.append(d_gate_up)
        normed_two_all.append(normed_two)
        branch_all.append(grad_branch)
        gain_two_sum = gain_two_sum + gain_two

    def rows(parts):
        return jnp.concatenate(parts, axis=0)

    grad_out = mm(jnp.concatenate(attended_all, axis=1), rows(branch_all), 1, 0).astype(BF)
    grad_in = mm(rows(normed_two_all), rows(d_gate_all), 0, 0).astype(BF)
    grad_down = mm(rows(hidden_all), cotangent.reshape(-1, width), 0, 0).astype(BF)
    slot_cap = master.shape[0]
    slot_total = slot_cap * ctx_size * lax.axis_size("fsdp")
    where = after(slot_table[3 * (width // 64) ** 2 :], d_att_all[0])
    fast = halving_applies() and micro == 2
    waits = [()] * micro
    if fast:
        owner = where // slot_cap
        rest = where % slot_cap
        cut = slot_cap // 2
        low = rest < cut
        core = (owner // 2) % 2
        x_rel = (owner % 2) ^ lax.axis_index("fsdp")
        ctx_rel = (owner // 2) ^ ctx_index
        y_rel, z_one, z_two = (ctx_rel // 2) % 2, (ctx_rel // 4) % 2, ctx_rel // 8
        z_rel = z_one * 2 + z_two
        place = jnp.where(
            low,
            ((x_rel * 2 + y_rel) * 4 + z_rel) * cut + rest,
            16 * cut + ((y_rel * 2 + x_rel) * 4 + z_rel) * (slot_cap - cut) + rest - cut,
        )
        where = place + jnp.where(core == ctx_index % 2, slot_total // 2, 0)
        send, keep = scatter_tiles([grad_out, grad_in, grad_down], where, slot_total, 2)
        got = swap_bit(send, "ctx", 1)

        def both(low, high):
            return keep[low:high] + got[low:high]

        ours = [both(0, 8 * cut), both(16 * cut, 16 * cut + 8 * (slot_cap - cut))]
        theirs = [both(8 * cut, 16 * cut), both(16 * cut + 8 * (slot_cap - cut), 16 * slot_cap)]
        near = [swap_bit(theirs[0], "fsdp", 1), swap_bit(theirs[1], "ctx", 2)]
        waits[0] = (*ours, *theirs)
    else:
        (slotted,) = scatter_tiles([grad_out, grad_in, grad_down], where, slot_total, 1)
        own_slots = lax.psum_scatter(slotted, ("ctx", "fsdp"), scatter_dimension=0, tiled=True)

    d_proj_all, grad_heads = [], 0.0
    for b in range(micro):
        cosine, sine = tables[b]
        d_att = after(d_att_all[b], *waits[b])
        grads, flat = attend_backward(
            qkv_all[b], segments[b], d_att, *raw_all[b], cosine, sine, bq=512, bk=512, sub=512
        )
        if fast and b == 0:
            near = [after(v, grads) for v in near]
            next_ours = [t[: t.shape[0] // 2] + v[: t.shape[0] // 2] for t, v in zip(ours, near)]
            next_theirs = [t[t.shape[0] // 2 :] + v[t.shape[0] // 2 :] for t, v in zip(ours, near)]
            next_near = [swap_bit(next_theirs[0], "ctx", 2), swap_bit(next_theirs[1], "fsdp", 1)]
            waits[1] = (*next_ours, *next_theirs)
        elif fast:
            next_near = [after(v, grads) for v in next_near]
            pair = [(t.reshape(2, 2, -1, 32, 128), v.reshape(2, 2, -1, 32, 128)) for t, v in zip(next_ours, next_near)]
            kept, sent = (jnp.concatenate([t[side] + v[side] for t, v in pair], axis=1) for side in (0, 1))
            flat = after(flat, sent)
            got = swap_bit(sent, "ctx", 4)
            kept, sent = (kept[side] + got[side] for side in (0, 1))
            first_turn = got
            own_slots = kept + swap_bit(sent, "ctx", 8)
        last_grads = grads
        if b + 1 < micro:
            d_proj_all.append(collect(grads))
        grad_heads = grad_heads + mm(flat, normed_wide[b], 1, 0)

    states = [master, first_moment, rotated_second_moments, row_eigenbasis, column_eigenbasis]
    outputs_list = [(m + mm(h, full_down, 1, 0)).astype(BF) for m, h in results]
    own, live = own_tiles(slot_table, slot_cap)
    is_qkv = own < 3 * heads * (width // 64)
    share = lax.dynamic_index_in_dim(full_qkv.reshape(width, 3, heads, HEAD), ctx_index // copies, 2, keepdims=False)
    gain_one = jnp.sum(grad_heads * share.reshape(width, 3 * HEAD).T.astype(F32), axis=0) / (gains[0] * copies)
    grad_heads = after(grad_heads.astype(BF), d_proj_all[0], *(next_near if fast else ()))
    if fast and heads == ctx_size:
        grad_heads = after(grad_heads + swap_bit(grad_heads, "fsdp", 1), first_turn)
        pool, place, first_round = send_tiles(slot_table, slot_cap, grad_heads, own)
        last_grads = after(last_grads, first_round, own_slots, pool[1], *outputs_list)
    else:
        grad_heads = lax.psum(grad_heads, "fsdp")
        pool = (all_tiles(lax.all_gather(grad_heads[None], "ctx", axis=0, tiled=True)[::copies]),) * 2
        place = own
    d_proj_all.append(collect(last_grads))
    picks = (is_qkv.astype(jnp.int32), jnp.where(is_qkv, place, 0), live)

    input_grads = []
    for b in range(micro):
        d_proj = d_proj_all[b].reshape(heads, 3, HEAD, shard).transpose(1, 0, 2, 3).reshape(3 * width, shard)
        d_normed = mm(d_proj, full_qkv, 0, 1)
        d_in_norm, _ = norm_back(layer_ins[b], gains[0], d_normed)
        input_grads.append((d_middles[b] + d_in_norm).astype(BF))
    gain_grads = sum_all(after(jnp.stack([gain_one, gain_two_sum]), d_proj_all[-1]))

    own_grads, new_master, new_copy, new_first, new_second = soap_step(
        picks, pool, own_slots, *states
    )
    new_gains, new_gain_first, new_gain_second = gain_step(gain_grads, gain_master, gain_first, gain_second)
    return (
        jnp.stack(outputs_list),
        jnp.stack(input_grads),
        own_grads,
        gain_grads,
        new_master,
        new_copy,
        new_first,
        new_second,
        new_gains,
        new_gain_first,
        new_gain_second,
    )


def solution(mesh):
    tokens = P("fsdp", "ctx", None)
    slots = P(("ctx", "fsdp"), None, None)
    placed = (
        tokens,
        tokens,
        *(P("fsdp", None),) * 5,
        P(None, "fsdp"),
        P(),
        *(slots,) * 5,
        *(P(),) * 3,
    )
    return jax.shard_map(
        on_device,
        mesh=mesh,
        in_specs=placed,
        out_specs=(tokens, tokens, slots, P(), slots, slots, slots, slots, P(), P(), P()),
        check_vma=False,
    )
```
